512 devices in a mesh: dom: 512 (over x, y, z, core).
Axes of the slice: x: 4, y: 4, z: 16, core: 2. Of those that a mesh axis runs over, the one named last changes fastest.
Arguments:
- counts: float32 [64, 262144], P(None, 'dom'), may hold values from 0.5 to 8
- scaled_rate_constants: float32 [256], replicated, may hold values from 0.001 to 0.05
- reactant_species_index: int32 [2, 256], replicated, may hold values from 0 to 64
- product_species_index: int32 [2, 256], replicated, may hold values from 0 to 64
- leap_gaussian_noise: bfloat16 [256, 262144], P(None, 'dom'), may hold values from -5 to 5
- diff_rates: float32 [64], replicated, may hold values from 0.01 to 0.2
- face_weights: float32 [4, 262144], P(None, 'dom'), may hold values from 0.2 to 1.2
- face_target: int32 [4, 262144], P(None, 'dom'), may hold values from 0 to 1024, as said below
- recv_rows: int32 [2, 131072], P(None, 'dom'), may hold values from 0 to 512, as said below
- diff_noise: bfloat16 [4, 64, 262144], P(None, None, 'dom'), may hold values from -5 to 5
- tri_tet: int32 [262144], P('dom'), may hold values from 0 to 511
- tri_verts: int32 [3, 262144], P(None, 'dom'), may hold values from 0 to 767, as said below
- tri_area: float32 [262144], P('dom'), may hold values from 0.5 to 1.5
- voltage_old: float32 [131072], P('dom')
- mass: float32 [131072], P('dom'), may hold values from 0.5 to 4
- mat_cols: int32 [8, 131072], P(None, 'dom'), may hold values from 0 to 767, as said below
- mat_vals: float32 [8, 131072], P(None, 'dom'), may hold values from -1 to -0.2
Outputs:
- counts_new: float32 [64, 262144], P(None, 'dom')
- voltage_new: float32 [131072], P('dom')
The draws below stay inside these ranges and needn't reach their ends.
Inputs may be any that keep to these rules, and one draw needn't show every extreme that they name: `face_target`: each entry is a tetrahedron of the same partition (below 512), send slot k = entry - 512 (slots below 256 lead to the partition before, the others to the partition after), or 1024 for a wall. Each send slot is named by at most one face. Send slot 256 + i of a partition and slot i of the partition after describe the same pair of tetrahedra, in opposite directions; the used slots towards a neighbour are the lowest ones; the first partition sends nothing before it and the last nothing after it. Some pair of neighbouring partitions is joined by exactly 256 faces. `recv_rows`: entry i of row 0 of a partition is the tetrahedron joined to send slot 256 + i of the partition before, entry i of row 1 the one joined to send slot i of the partition after, or 512 where that slot is unused; the entries of one row of one partition that are below 512 are distinct. `tri_verts`: the first partition names no vertex before it, the last none after it. `mat_cols`: encoded as tri_verts. Slots 0, 1, 4, 5 name vertices of the own partition, slots 2, 3 of the partition after, slots 6, 7 of the partition before; with mat_vals the off-diagonal entries between existing vertices are symmetric.
All inputs are finite; a program needn't handle non-finite values.
Results may differ from the reference program's by a relative error of at most 0.0003.
Values sent between devices are 32-bit elements; how exact they have to be, the bound alone decides.
A program may use at most 64 MiB of HBM per device.

```python
import math
import jax
import jax.numpy as jnp
from jax import lax

S = 64
R = 256
TET_DEV = 512
BND = 256
TRI_DEV = 512
V_DEV = 256
K = 8
ITERS = 2
TETS = 262144
TRIS = 262144
VERTS = 131072
N_DOM = 512


def chain_structure(key):
    devices = TETS // TET_DEV
    base_key = jax.random.fold_in(key, 11)
    subkeys = jax.random.split(base_key, 3)
    full_pair = jax.random.randint(subkeys[0], (), 0, devices - 1)
    pair_faces = jax.random.randint(subkeys[1], (devices,), BND // 4, BND + 1)
    positions = jnp.arange(devices, dtype=jnp.int32)
    pair_faces = jnp.where(positions == full_pair, BND, pair_faces)
    pair_faces = jnp.where(positions == devices - 1, 0, pair_faces)
    faces_before = jnp.concatenate([jnp.zeros((1,), jnp.int32), pair_faces[:-1]])
    device_keys = jax.random.split(subkeys[2], devices)

    def per_device(device_key, count_before, count_after):
        inner_keys = jax.random.split(device_key, 4)
        left_tets = jax.random.permutation(inner_keys[0], TET_DEV)[:BND].astype(jnp.int32)
        right_tets = jax.random.permutation(inner_keys[1], TET_DEV)[:BND].astype(jnp.int32)
        own_tets = jnp.arange(TET_DEV, dtype=jnp.int32)
        offsets = jax.random.randint(inner_keys[2], (4, TET_DEV), 1, TET_DEV)
        targets = (own_tets[None, :] + offsets) % TET_DEV
        wall_draw = jax.random.randint(inner_keys[3], (4, TET_DEV), 0, 4) == 0
        face_rows = jnp.arange(4, dtype=jnp.int32)[:, None]
        targets = jnp.where(wall_draw & (face_rows >= 2), TET_DEV + 2 * BND, targets)
        slot_index = jnp.arange(BND, dtype=jnp.int32)
        left_used = jnp.where(slot_index < count_before, left_tets, TET_DEV)
        right_used = jnp.where(slot_index < count_after, right_tets, TET_DEV)
        targets = targets.at[2, left_used].set(TET_DEV + slot_index, mode='drop')
        targets = targets.at[3, right_used].set(TET_DEV + BND + slot_index, mode='drop')
        return (targets, jnp.stack([left_used, right_used]))
    all_targets, all_rows = jax.vmap(per_device)(device_keys, faces_before, pair_faces)
    face_target = all_targets.transpose(1, 0, 2).reshape(4, devices * TET_DEV)
    recv_lists = all_rows.transpose(1, 0, 2).reshape(2, devices * BND)
    return (face_target.astype(jnp.int32), recv_lists.astype(jnp.int32))


def draw_face_target(key, part):
    return chain_structure(key)[0]


def draw_recv_rows(key, part):
    return chain_structure(key)[1]


def draw_tri_verts(key, part):
    devices = TRIS // TRI_DEV
    subkeys = jax.random.split(jax.random.fold_in(key, 23), 2)
    block_draw = jax.random.randint(subkeys[0], (3, TRIS), 0, 8)
    side_index = jnp.where(block_draw == 0, 0, jnp.where(block_draw == 1, 2, 1))
    owner = jnp.arange(TRIS, dtype=jnp.int32) // TRI_DEV
    side_index = jnp.where((owner == 0)[None, :] & (side_index == 0), 1, side_index)
    side_index = jnp.where((owner == devices - 1)[None, :] & (side_index == 2), 1, side_index)
    local_vertex = jax.random.randint(subkeys[1], (3, TRIS), 0, V_DEV)
    return (side_index * V_DEV + local_vertex).astype(jnp.int32)


def matrix_structure(key):
    devices = VERTS // V_DEV
    base_key = jax.random.fold_in(key, 37)
    perm_keys = jax.random.split(base_key, 4 * devices)
    perms = jax.vmap(lambda perm_key: jax.random.permutation(perm_key, V_DEV))(perm_keys)
    perms = perms.reshape(4, devices, V_DEV).astype(jnp.int32)
    inverse = jnp.argsort(perms, axis=-1, stable=True).astype(jnp.int32)
    weights = jax.random.uniform(jax.random.fold_in(base_key, 1), (4, devices, V_DEV), jnp.float32, 0.2, 1.0)
    column_list = []
    value_list = []
    for slot_number in range(4):
        block_start = V_DEV if slot_number < 2 else 2 * V_DEV
        column_list.append(block_start + perms[slot_number])
        value_list.append(-weights[slot_number])
    for slot_number in range(4):
        if slot_number < 2:
            column_list.append(V_DEV + inverse[slot_number])
            value_list.append(-jnp.take_along_axis(weights[slot_number], inverse[slot_number], axis=1))
        else:
            inverse_prev = jnp.roll(inverse[slot_number], 1, axis=0)
            weights_prev = jnp.roll(weights[slot_number], 1, axis=0)
            column_list.append(inverse_prev)
            value_list.append(-jnp.take_along_axis(weights_prev, inverse_prev, axis=1))
    columns = jnp.stack(column_list).reshape(8, devices * V_DEV)
    values = jnp.stack(value_list).reshape(8, devices * V_DEV)
    return (columns.astype(jnp.int32), values.astype(jnp.float32))


def draw_mat_cols(key, part):
    return matrix_structure(key)[0]


def draw_mat_vals(key, part):
    return matrix_structure(key)[1]


def draw_voltage_old(key, part):
    devices = VERTS // V_DEV
    subkeys = jax.random.split(jax.random.fold_in(key, 41), 2)
    owner = (jnp.arange(VERTS, dtype=jnp.int32) // V_DEV).astype(jnp.float32)
    ramp = 1.0 + 2.0 * owner / max(devices - 1, 1)
    spread_scale = jnp.exp(jax.random.uniform(subkeys[0], (VERTS,), jnp.float32, 0.0, 2.302585))
    base_values = jax.random.normal(subkeys[1], (VERTS,), jnp.float32)
    return 0.2 * base_values * spread_scale * ramp


def plant(entries, rng, smallest, high):
    longest = entries.shape.index(max(entries.shape))
    spots = []
    for shift in (0, 1):
        where = [jax.random.randint(jax.random.fold_in(rng, axis), (), 0, length) for axis, length in enumerate(entries.shape)]
        where[longest] = (where[longest] + shift) % entries.shape[longest]
        spots.append(tuple(where))
    return entries.at[spots[0]].set(smallest).at[spots[1]].set(high)


def block_scale(own_key, extent, shards, low, largest):
    gain = 1.0
    for axis_at, shards_of in shards:
        draws = jax.random.uniform(jax.random.fold_in(jax.random.fold_in(own_key, 6), axis_at), (shards_of,), jnp.float32, low / len(shards), largest / len(shards))
        gain = gain * jnp.repeat(jnp.exp(draws), extent[axis_at] // shards_of).reshape((-1,) + (1,) * (len(extent) - 1 - axis_at))
    return gain


def noise(rng, extent, scale, bound, pieces=(), kind=jnp.bfloat16):
    factor_of = block_scale(rng, extent, pieces, -0.22, 0.18) if pieces else 1.0
    result = jax.random.normal(rng, extent, jnp.float32) * scale * factor_of
    return jnp.minimum(jnp.maximum(result, -bound), bound).astype(kind)


def setup_inputs(seed: int = 0) -> dict:
    streams_of = jax.random.split(jax.random.key(seed), 18)
    return {
        "counts": jnp.clip(0.5 + 7.5 * jax.random.uniform(streams_of[0], (S, TETS), jnp.float32) ** block_scale(streams_of[0], (S, TETS), ((1, 512),), -0.2, 0.2), 0.5, 8.0),
        "scaled_rate_constants": jnp.clip(jnp.exp(jax.random.uniform(streams_of[1], (R,), jnp.float32, math.log(0.001), math.log(0.05))), 0.001, 0.05),
        "reactant_species_index": plant(jax.random.randint(streams_of[2], (2, R), 0, S + 1), jax.random.fold_in(streams_of[2], 1), 0, S).astype(jnp.int32),
        "product_species_index": plant(jax.random.randint(streams_of[3], (2, R), 0, S + 1), jax.random.fold_in(streams_of[3], 1), 0, S).astype(jnp.int32),
        "leap_gaussian_noise": noise(streams_of[4], (R, TETS), 1.0, 5.0, ((1, 512),)),
        "diff_rates": jnp.clip(jnp.exp(jax.random.uniform(streams_of[5], (S,), jnp.float32, math.log(0.01), math.log(0.2))), 0.01, 0.2),
        "face_weights": jnp.clip(0.2 + 1 * jax.random.uniform(streams_of[6], (4, TETS), jnp.float32) ** block_scale(streams_of[6], (4, TETS), ((1, 512),), -0.2, 0.2), 0.2, 1.2),
        "face_target": draw_face_target(jax.random.fold_in(streams_of[17], 71), 0),
        "recv_rows": draw_recv_rows(jax.random.fold_in(streams_of[17], 71), 0),
        "diff_noise": noise(streams_of[9], (4, S, TETS), 1.0, 5.0, ((2, 512),)),
        "tri_tet": plant(jax.random.randint(streams_of[10], (TRIS,), 0, TET_DEV), jax.random.fold_in(streams_of[10], 1), 0, TET_DEV - 1).astype(jnp.int32),
        "tri_verts": draw_tri_verts(jax.random.fold_in(streams_of[17], 71), 0),
        "tri_area": jnp.clip(0.5 + 1.0 * jax.random.uniform(streams_of[12], (TRIS,), jnp.float32) ** block_scale(streams_of[12], (TRIS,), ((0, 512),), -0.2, 0.2), 0.5, 1.5),
        "voltage_old": draw_voltage_old(jax.random.fold_in(streams_of[17], 71), 0),
        "mass": jnp.clip(jnp.exp(math.log(4.0) - 2.0794415 * jax.random.uniform(streams_of[14], (VERTS,), jnp.float32) ** block_scale(streams_of[14], (VERTS,), ((0, 512),), -0.2, 0.2)), 0.5, 4.0),
        "mat_cols": draw_mat_cols(jax.random.fold_in(streams_of[17], 71), 0),
        "mat_vals": draw_mat_vals(jax.random.fold_in(streams_of[17], 71), 0),
    }


BIG_LIMIT = 1e+30
CURRENT_GAIN = 4.0
HALF_SATURATION = 2.0

def tau_leap_events(partial_counts, scaled_rate_constants, reactant_species_index, partial_noise):
    species = partial_counts.shape[0]
    extended = jnp.concatenate([partial_counts, jnp.ones((1, partial_counts.shape[1]), jnp.float32)], axis=0)
    first_in = jnp.take(extended, reactant_species_index[0], axis=0)
    second_in = jnp.take(extended, reactant_species_index[1], axis=0)
    propensity = scaled_rate_constants[:, None] * first_in * second_in
    limit_first = jnp.where((reactant_species_index[0] < species)[:, None], first_in, BIG_LIMIT)
    limit_second = jnp.where((reactant_species_index[1] < species)[:, None], second_in, BIG_LIMIT)
    limit_all = jnp.minimum(limit_first, limit_second)
    raw_leap = propensity + jnp.sqrt(propensity) * partial_noise.astype(jnp.float32)
    return jnp.minimum(jnp.maximum(raw_leap, 0.0), limit_all)

def diffusion_amounts(reacted, diff_rates, weights, targets, partial_noise, wall_slot):
    hop_prob = diff_rates[None, :, None] * weights[:, None, :]
    mean_hop = reacted[None, :, :] * hop_prob
    spread_hop = jnp.sqrt(mean_hop * (1.0 - hop_prob))
    raw_hop = jnp.maximum(mean_hop + spread_hop * partial_noise.astype(jnp.float32), 0.0)
    raw_hop = jnp.where((targets == wall_slot)[:, None, :], 0.0, raw_hop)
    total_out = lax.optimization_barrier(jnp.sum(raw_hop, axis=0))
    factor = jnp.minimum(1.0, reacted / jnp.maximum(total_out, 1.0))
    return raw_hop * factor[None, :, :]

def deposit_faces(amount, targets, width):
    buffer = jnp.zeros((amount.shape[1], width), jnp.float32)
    for face_index in range(4):
        buffer = buffer.at[:, targets[face_index]].add(amount[face_index])
    return buffer

def reference(counts, scaled_rate_constants, reactant_species_index, product_species_index, leap_gaussian_noise, diff_rates, face_weights, face_target, recv_rows, diff_noise, tri_tet, tri_verts, tri_area, voltage_old, mass, mat_cols, mat_vals):
    wall_slot = TET_DEV + 2 * BND

    def local_phase(device_index):
        first_col = device_index * TET_DEV
        partial_counts = lax.dynamic_slice_in_dim(counts, first_col, TET_DEV, 1)
        partial_noise = lax.dynamic_slice_in_dim(leap_gaussian_noise, first_col, TET_DEV, 1)
        weights = lax.dynamic_slice_in_dim(face_weights, first_col, TET_DEV, 1)
        targets = lax.dynamic_slice_in_dim(face_target, first_col, TET_DEV, 1)
        dnoise = lax.dynamic_slice_in_dim(diff_noise, first_col, TET_DEV, 2)
        reaction_events = tau_leap_events(partial_counts, scaled_rate_constants, reactant_species_index, partial_noise)
        count_delta = jnp.zeros((S + 1, TET_DEV), jnp.float32)
        count_delta = count_delta.at[product_species_index[0]].add(reaction_events).at[product_species_index[1]].add(reaction_events)
        count_delta = count_delta.at[reactant_species_index[0]].add(-reaction_events).at[reactant_species_index[1]].add(-reaction_events)
        reacted = jnp.maximum(partial_counts + count_delta[:S], 0.0)
        amount = diffusion_amounts(reacted, diff_rates, weights, targets, dnoise, wall_slot)
        remaining = reacted - lax.optimization_barrier(jnp.sum(amount, axis=0))
        buffer = deposit_faces(amount, targets, wall_slot + 1)
        return (remaining + buffer[:, :TET_DEV], buffer[:, TET_DEV:wall_slot])
    local_all, send_all = lax.map(local_phase, jnp.arange(N_DOM, dtype=jnp.int32))
    zero_block = jnp.zeros((1, S, BND), jnp.float32)
    from_before = jnp.concatenate([zero_block, send_all[:-1, :, BND:]], axis=0)
    from_after = jnp.concatenate([send_all[1:, :, :BND], zero_block], axis=0)
    recv_lists = recv_rows.reshape(2, N_DOM, BND)

    def receive(local_part, before_part, after_part, row_before, row_after):
        padded = jnp.concatenate([local_part, jnp.zeros((S, 1), jnp.float32)], axis=1)
        padded = padded.at[:, row_before].add(before_part).at[:, row_after].add(after_part)
        return padded[:, :TET_DEV]
    final = jax.vmap(receive)(local_all, from_before, from_after, recv_lists[0], recv_lists[1])
    counts_new = final.transpose(1, 0, 2).reshape(S, N_DOM * TET_DEV)
    calcium_all = final[:, 0, :]
    calcium = jnp.take_along_axis(calcium_all, tri_tet.reshape(N_DOM, TRI_DEV), axis=1)
    share_each = CURRENT_GAIN * tri_area.reshape(N_DOM, TRI_DEV) * calcium / (calcium + HALF_SATURATION) / 3.0
    corners = tri_verts.reshape(3, N_DOM, TRI_DEV)

    def deposit_vertices(values, corner_a, corner_b, corner_c):
        buffer = jnp.zeros((3 * V_DEV,), jnp.float32)
        return buffer.at[corner_a].add(values).at[corner_b].add(values).at[corner_c].add(values)
    spread_all = jax.vmap(deposit_vertices)(share_each, corners[0], corners[1], corners[2])
    zero_row = jnp.zeros((1, V_DEV), jnp.float32)
    injected = spread_all[:, V_DEV:2 * V_DEV] + jnp.concatenate([zero_row, spread_all[:-1, 2 * V_DEV:]], axis=0)
    injected = injected + jnp.concatenate([spread_all[1:, :V_DEV], zero_row], axis=0)
    rhs = mass * voltage_old + injected.reshape(-1)
    cols_dev = mat_cols.reshape(K, N_DOM, V_DEV).transpose(1, 0, 2)
    vals_dev = mat_vals.reshape(K, N_DOM, V_DEV).transpose(1, 0, 2)
    diagonal = mass.reshape(N_DOM, V_DEV) + lax.optimization_barrier(jnp.sum(jnp.abs(vals_dev), axis=1))

    def pick_values(extended_row, column_row):
        return extended_row[column_row]

    def operate(field):
        grid = field.reshape(N_DOM, V_DEV)
        extended = jnp.concatenate([jnp.concatenate([zero_row, grid[:-1]], axis=0), grid, jnp.concatenate([grid[1:], zero_row], axis=0)], axis=1)
        taken = jax.vmap(pick_values)(extended, cols_dev)
        return (diagonal * grid + lax.optimization_barrier(jnp.sum(vals_dev * taken, axis=1))).reshape(-1)
    solution = voltage_old
    residual = rhs - operate(voltage_old)
    direction = residual
    norm_now = jnp.sum(residual * residual)
    for turn_index in range(ITERS):
        image = operate(direction)
        alpha = norm_now / jnp.sum(direction * image)
        solution = solution + alpha * direction
        residual = residual - alpha * image
        norm_next = jnp.sum(residual * residual)
        direction = residual + norm_next / norm_now * direction
        norm_now = norm_next
    return (counts_new, solution)
```

```python
import jax
import jax.numpy as jnp
from jax import lax
from jax.experimental import pallas as pl
from jax.experimental.pallas import tpu as pltpu
from jax.sharding import PartitionSpec as P

F32 = jnp.float32
BF16 = jnp.bfloat16
I32 = jnp.int32
MESH = pl.DeviceIdType.MESH

N = 512
S = 64
R = 256
T = 512
B = 256
V = 256
BIG = 1e30
SCALE = 1.0 / 32.0
ZG = 32
XY = 16


def nn(a, b):
    return lax.dot_general(a, b, (((1,), (0,)), ((), ())), preferred_element_type=F32)


def nt(a, b):
    return lax.dot_general(a, b, (((1,), (1,)), ((), ())), preferred_element_type=F32)


def iota(shape, dim):
    return lax.broadcasted_iota(I32, shape, dim)


def cut2(x):
    hi = x.astype(BF16)
    return hi, (x - hi.astype(F32)).astype(BF16)


def cut3(x):
    hi = x.astype(BF16)
    rest = x - hi.astype(F32)
    mid = rest.astype(BF16)
    return hi, mid, (rest - mid.astype(F32)).astype(BF16)


def rows3(x):
    hi = x.astype(BF16).astype(F32)
    rest = x - hi
    mid = rest.astype(BF16).astype(F32)
    low = rest - mid
    at = iota((16, x.shape[1]), 0)
    return jnp.where(at == 0, hi, jnp.where(at == 1, mid, jnp.where(at == 2, low, 0.0))).astype(BF16)


def add_rows(x):
    return jnp.sum(x, axis=0, keepdims=True)


def column(row, size):
    return jnp.sum(
        jnp.where(iota((size, size), 0) == iota((size, size), 1), row, 0.0), axis=1, keepdims=True
    )


def hot(cond):
    return jnp.where(cond, 1.0, 0.0).astype(BF16)


def build_matrix(cols, vals, mass, keep_before, keep_after, hi_ref, lo_ref):
    diag = (mass[...] + jnp.sum(jnp.abs(vals[...]), axis=0, keepdims=True)) * SCALE
    step = 64
    for block, slots in ((0, (6, 7)), (1, (0, 1, 4, 5)), (2, (2, 3))):
        for j0 in range(0, V, step):
            at = iota((step, V), 0) + (block * V + j0)
            total = jnp.zeros((step, V), F32)
            for k in slots:
                total = total + jnp.where(cols[k : k + 1, :] == at, vals[k : k + 1, :] * SCALE, 0.0)
            if block == 0:
                total = total * keep_before
            elif block == 2:
                total = total * keep_after
            else:
                total = total + jnp.where(iota((step, V), 1) == at - V, diag, 0.0)
            hi, lo = cut2(total)
            hi_ref[block * V + j0 : block * V + j0 + step, :] = hi
            lo_ref[block * V + j0 : block * V + j0 + step, :] = lo


def kernel(
    counts_h, rate_h, ri_h, pi_h, leap_h, dr_h, fw_h, ft_h, rr_h, dn_h, tt_h, tv_h, ta_h, v_h, m_h, mc_h, mv_h,
    out_h, vout_h,
    counts, rate, ri, pi, leap, dr, fw, ft, rrow, dn, tt, tv, ta, v, m, mc, mv,
    xs, fire, am, ot, loc, rt, gt, ct, bh, bl, nh, nl, arr, cnew, vnew,
    slots, slots_in, pk1, rx1, nc, nv, nm, pk2, rx2, red, red_a, red_b,
    in_sem, out_sem, send_sem, recv_sem,
):
    me = lax.axis_index("dom")
    hbm = (counts_h, rate_h, ri_h, pi_h, leap_h, dr_h, fw_h, ft_h, rr_h, dn_h, tt_h, tv_h, ta_h, v_h, m_h, mc_h, mv_h)
    vmem = (counts, rate, ri, pi, leap, dr, fw, ft, rrow, dn, tt, tv, ta, v, m, mc, mv)
    loads = [pltpu.make_async_copy(h, d, in_sem.at[i]) for i, (h, d) in enumerate(zip(hbm, vmem))]
    for i in (7, 2, 3, 1, 0, 4, 5, 6, 9, 8, 10, 11, 12, 13, 14, 15, 16):
        loads[i].start()

    def chain(offset):
        return lax.rem(me + (offset + N), N)

    z_base = (me // ZG) * ZG
    z_at = lax.rem(me, ZG)
    xy_at = me // ZG

    def z_partner(j):
        return z_base + lax.rem(z_at + j, ZG)

    def xy_partner(j):
        return lax.rem(xy_at + j, XY) * ZG + z_at

    barrier = pltpu.get_barrier_semaphore()
    greet = [chain(o) for o in (1, -1, 2, -2, 3, -3)]
    greet += [z_partner(j) for j in range(1, ZG)] + [xy_partner(j) for j in range(1, XY)]
    for other in greet:
        pl.semaphore_signal(barrier, inc=1, device_id=(other,), device_id_type=MESH)

    loads[7].wait()

    def build_targets(c, carry):
        at = iota((64, T), 0) + c * 64
        start = pl.multiple_of(c * 64, 64)
        for f in range(4):
            ot[pl.ds(start, 64), f * T : (f + 1) * T] = hot(ft[f : f + 1, :] == at)
        return carry

    lax.fori_loop(0, (T + 2 * B) // 64, build_targets, 0)

    for i in (0, 1, 2, 3, 4):
        loads[i].wait()
    for i, part in enumerate(cut3(counts[...])):
        xs[i * S : (i + 1) * S, :] = part
    xs[3 * S :, :] = jnp.ones((S, T), BF16)
    lane = iota((1, 256), 1)
    wanted = jnp.where(lane < 3 * S, lax.rem(lane, S), jnp.where(lane == 3 * S, S, -1)).astype(F32)
    first = column(ri[0:1, :].astype(F32), R)
    second = column(ri[1:2, :].astype(F32), R)
    rates = column(rate[...], R)
    cap_first = jnp.where(first == S, BIG, 0.0)
    cap_second = jnp.where(second == S, BIG, 0.0)
    step = 64
    for c in range(0, R, step):
        one = first[c : c + step, :]
        two = second[c : c + step, :]
        x1 = nn(hot(one == wanted), xs[...])
        x2 = nn(hot(two == wanted), xs[...])
        prop = rates[c : c + step, :] * x1 * x2
        limit = jnp.minimum(
            jnp.maximum(x1, cap_first[c : c + step, :]), jnp.maximum(x2, cap_second[c : c + step, :])
        )
        raw = prop + jnp.sqrt(prop) * leap[c : c + step, :].astype(F32)
        hi, lo = cut2(jnp.minimum(jnp.maximum(raw, 0.0), limit))
        fire[c : c + step, :] = hi
        fire[R + c : R + c + step, :] = lo
    level = iota((S, R), 0)

    def has(row):
        return jnp.where(row == level, 1.0, 0.0)

    stoich = (has(pi[0:1, :]) + has(pi[1:2, :]) - has(ri[0:1, :]) - has(ri[1:2, :])).astype(BF16)
    delta = nn(stoich, fire[0:R, :]) + nn(stoich, fire[R:, :])
    cnew[...] = jnp.maximum(counts[...] + delta, 0.0)

    for i in (5, 6, 9):
        loads[i].wait()
    hop = column(dr[...], S)
    step = 16
    for c in range(0, S, step):
        here = cnew[c : c + step, :]
        raws = []
        for f in range(4):
            prob = hop[c : c + step, :] * fw[f : f + 1, :]
            mean = here * prob
            spread = jnp.sqrt(mean * (1.0 - prob))
            raw = jnp.maximum(mean + spread * dn[f, c : c + step, :].astype(F32), 0.0)
            raws.append(jnp.where(ft[f : f + 1, :] == T + 2 * B, 0.0, raw))
        total = raws[0] + raws[1] + raws[2] + raws[3]
        factor = jnp.minimum(1.0, here / jnp.maximum(total, 1.0))
        for f in range(4):
            hi, lo = cut2(raws[f] * factor)
            am[c : c + step, f * T : (f + 1) * T] = hi
            am[S + c : S + c + step, f * T : (f + 1) * T] = lo
        loc[c : c + step, :] = here - total * factor
    for side in range(2):
        out = nt(am[...], ot[T + side * B : T + (side + 1) * B, :])
        slots[side] = out[:S, :] + out[S:, :]
    loads[13].wait()
    for side in range(2):
        pk1[side, :, 0:B] = slots[side, 0:1, :]
        pk1[side, :, B:] = v[...]

    for i in (14, 15, 16):
        loads[i].wait()
    pl.semaphore_wait(barrier, len(greet))
    sends = []

    def send(src, dst, sem, other):
        copy = pltpu.make_async_remote_copy(
            src_ref=src, dst_ref=dst, send_sem=send_sem.at[sem], recv_sem=recv_sem.at[sem],
            device_id=(other,), device_id_type=MESH,
        )
        copy.start()
        sends.append(copy)
        return copy

    before, after = chain(-1), chain(1)
    small = [send(pk1.at[1], rx1.at[0], 0, after), send(pk1.at[0], rx1.at[1], 1, before)]
    params = [send(mc, nc, 2, before), send(mv, nv, 3, before), send(m, nm, 4, before)]
    bulk = [send(slots.at[1], slots_in.at[0], 5, after), send(slots.at[0], slots_in.at[1], 6, before)]

    for w in range(0, T, 256):
        out = nt(am[...], ot[w : w + 256, :])
        loc[:, w : w + 256] = loc[:, w : w + 256] + out[:S, :] + out[S:, :]
    loads[8].wait()
    loads[10].wait()
    loads[11].wait()
    loads[12].wait()
    for c in range(0, T, 64):
        at = iota((64, B), 0) + c
        rt[c : c + 64, 0:B] = hot(rrow[0:1, :] == at)
        rt[c : c + 64, B:] = hot(rrow[1:2, :] == at)
        gt[c : c + 64, :] = hot(tt[...] == iota((64, T), 0) + c)
    for c in range(0, 3 * V, 64):
        at = iota((64, T), 0) + c
        total = jnp.where(tv[0:1, :] == at, 1.0, 0.0)
        total = total + jnp.where(tv[1:2, :] == at, 1.0, 0.0)
        total = total + jnp.where(tv[2:3, :] == at, 1.0, 0.0)
        ct[c : c + 64, :] = total.astype(BF16)

    def flag(cond):
        return jnp.where(cond, 1.0, 0.0).astype(F32)

    has_before, has_after = flag(me > 0), flag(me < N - 1)
    build_matrix(mc, mv, m, has_before, has_after, bh, bl)

    def apply(x, hi_ref, lo_ref, start=0):
        parts = rows3(x)
        size = x.shape[1]
        out = nn(parts, hi_ref[start : start + size, :]) + nn(parts, lo_ref[start : start + size, :])
        return add_rows(out)

    for copy in small:
        copy.wait_recv()
    arrived = jnp.concatenate([rx1[0, :, 0:B], rx1[1, :, 0:B]], axis=1)
    c0 = loc[0:1, :] + add_rows(nt(rows3(arrived), rt[...]))
    calcium = add_rows(nn(rows3(c0), gt[...]))
    share = 4.0 * ta[...] * calcium / (calcium + 2.0) / 3.0
    given = add_rows(nt(rows3(share), ct[...]))
    around = jnp.concatenate([rx1[0, :, B:], v[...], rx1[1, :, B:]], axis=1)
    start = m[...] * v[...] - apply(around, bh, bl) * (1.0 / SCALE)
    pk2[:, 0:V] = start + given[:, V : 2 * V]
    pk2[:, V : 2 * V] = given[:, 0:V]
    pk2[:, 2 * V :] = given[:, 2 * V :]

    parts2 = [send(pk2, rx2.at[i], 7 + i, chain(-o)) for i, o in enumerate((-2, -1, 1, 2, 3))]

    for copy in params:
        copy.wait_recv()
    build_matrix(nc, nv, nm, 1.0, flag(me < N - 2), nh, nl)
    for copy in parts2:
        copy.wait_recv()
    own_e, own_b, own_a = pk2[:, 0:V], pk2[:, V : 2 * V], pk2[:, 2 * V :]
    r_own = own_e + rx2[1, :, 2 * V :] + rx2[2, :, V : 2 * V]
    r_before = rx2[1, :, 0:V] + own_b + rx2[0, :, 2 * V :]
    r_after = rx2[2, :, 0:V] + own_a + rx2[3, :, V : 2 * V]
    r_after2 = rx2[3, :, 0:V] + rx2[2, :, 2 * V :] + rx2[4, :, V : 2 * V]
    u_own = apply(jnp.concatenate([r_before, r_own, r_after], axis=1), bh, bl)
    u_after = apply(jnp.concatenate([r_own, r_after, r_after2], axis=1), nh, nl)
    t_own = apply(jnp.concatenate([u_own, 2.0 * u_after], axis=1), bh, bl, V)

    def fold(x):
        return x[:, 0:128] + x[:, 128:256]

    products = (fold(r_own * r_own), fold(r_own * u_own), fold(u_own * u_own), fold(u_own * t_own))
    at = iota((8, 128), 0)
    stack = jnp.zeros((8, 128), F32)
    for i, p in enumerate(products):
        stack = jnp.where(at == i, p, stack)
    sums = jnp.sum(stack, axis=1, keepdims=True)
    red[0] = add_rows(jnp.where(at == iota((8, 128), 1), sums, 0.0))

    def reduce(stage, partner, size, buffer, sem):
        def go(j, carry):
            pltpu.make_async_remote_copy(
                src_ref=red.at[stage], dst_ref=buffer.at[j - 1], send_sem=send_sem.at[sem],
                recv_sem=recv_sem.at[sem], device_id=(partner(j),), device_id_type=MESH,
            ).start()
            return carry

        lax.fori_loop(1, size, go, 0, unroll=True)

    reduce(0, z_partner, ZG, red_a, 12)

    for copy in bulk:
        copy.wait_recv()
    for side in range(2):
        hi, lo = cut2(slots_in[side])
        arr[0:S, side * B : (side + 1) * B] = hi
        arr[S:, side * B : (side + 1) * B] = lo
    for w in range(0, T, 256):
        out = nt(arr[...], rt[w : w + 256, :])
        cnew[:, w : w + 256] = loc[:, w : w + 256] + out[:S, :] + out[S:, :]
    out_copy = pltpu.make_async_copy(cnew, out_h, out_sem.at[0])
    out_copy.start()

    pltpu.make_async_copy(red_a, red_a, recv_sem.at[12]).wait()
    red[1] = red[0] + jnp.sum(red_a[...], axis=0)
    reduce(1, xy_partner, XY, red_b, 13)
    pltpu.make_async_copy(red_b, red_b, recv_sem.at[13]).wait()
    final = red[1] + jnp.sum(red_b[...], axis=0)
    rr, ru, uu, ut = (final[:, i : i + 1] for i in range(4))
    alpha0 = rr / ru
    norm1 = alpha0 * alpha0 * uu - rr
    keep = 1.0 + norm1 / rr
    curve = keep * keep * ru - 2.0 * keep * alpha0 * uu + alpha0 * alpha0 * ut
    alpha1 = norm1 / curve
    direction = keep * r_own - alpha0 * u_own
    vnew[...] = v[...] + (alpha0 * SCALE) * r_own + (alpha1 * SCALE) * direction
    v_copy = pltpu.make_async_copy(vnew, vout_h, out_sem.at[1])
    v_copy.start()
    for copy in sends:
        copy.wait_send()
    pltpu.make_async_copy(red_a, red_a, send_sem.at[12]).wait()
    pltpu.make_async_copy(red_b, red_b, send_sem.at[13]).wait()
    out_copy.wait()
    v_copy.wait()


def per_device(*args):
    shaped = [a.reshape(1, -1) if a.ndim == 1 else a for a in args]
    any_spec = pl.BlockSpec(memory_space=pl.ANY)
    scratch = [pltpu.VMEM(a.shape, a.dtype) for a in shaped]
    scratch += [
        pltpu.VMEM((256, T), BF16),
        pltpu.VMEM((2 * R, T), BF16),
        pltpu.VMEM((2 * S, 4 * T), BF16),
        pltpu.VMEM((T + 2 * B, 4 * T), BF16),
        pltpu.VMEM((S, T), F32),
        pltpu.VMEM((T, 2 * B), BF16),
        pltpu.VMEM((T, T), BF16),
        pltpu.VMEM((3 * V, T), BF16),
        pltpu.VMEM((3 * V, V), BF16),
        pltpu.VMEM((3 * V, V), BF16),
        pltpu.VMEM((3 * V, V), BF16),
        pltpu.VMEM((3 * V, V), BF16),
        pltpu.VMEM((2 * S, 2 * B), BF16),
        pltpu.VMEM((S, T), F32),
        pltpu.VMEM((1, V), F32),
        pltpu.VMEM((2, S, B), F32),
        pltpu.VMEM((2, S, B), F32),
        pltpu.VMEM((2, 1, B + V), F32),
        pltpu.VMEM((2, 1, B + V), F32),
        pltpu.VMEM((8, V), I32),
        pltpu.VMEM((8, V), F32),
        pltpu.VMEM((1, V), F32),
        pltpu.VMEM((1, 3 * V), F32),
        pltpu.VMEM((5, 1, 3 * V), F32),
        pltpu.VMEM((2, 1, 128), F32),
        pltpu.VMEM((ZG - 1, 1, 128), F32),
        pltpu.VMEM((XY - 1, 1, 128), F32),
        pltpu.SemaphoreType.DMA((17,)),
        pltpu.SemaphoreType.DMA((2,)),
        pltpu.SemaphoreType.DMA((14,)),
        pltpu.SemaphoreType.DMA((14,)),
    ]
    counts_new, voltage = pl.pallas_call(
        kernel,
        name="step",
        out_shape=(jax.ShapeDtypeStruct((S, T), F32), jax.ShapeDtypeStruct((1, V), F32)),
        in_specs=[any_spec] * len(shaped),
        out_specs=(any_spec, any_spec),
        scratch_shapes=scratch,
        compiler_params=pltpu.CompilerParams(
            collective_id=1, has_side_effects=True, vmem_limit_bytes=60 * 1024 * 1024
        ),
    )(*shaped)
    return counts_new, voltage.reshape(-1)


def solution(mesh):
    placed = (
        P(None, "dom"), P(), P(), P(), P(None, "dom"), P(), P(None, "dom"), P(None, "dom"), P(None, "dom"),
        P(None, None, "dom"), P("dom"), P(None, "dom"), P("dom"), P("dom"), P("dom"), P(None, "dom"),
        P(None, "dom"),
    )
    return jax.shard_map(
        per_device, mesh=mesh, in_specs=placed, out_specs=(P(None, "dom"), P("dom")), check_vma=False
    )
```

```python
import jax
import jax.numpy as jnp
from jax import lax
from jax.experimental import pallas as pl
from jax.experimental.pallas import tpu as pltpu
from jax.sharding import PartitionSpec as P

F32 = jnp.float32
BF16 = jnp.bfloat16
I32 = jnp.int32
MESH = pl.DeviceIdType.MESH

N = 512
S = 64
R = 256
T = 512
B = 256
V = 256
BIG = 1e30
SCALE = 1.0 / 32.0
ZG = 32
XY = 16


HOPS = 4
PIECES = 2
NEAR_Z = [h for d in range(HOPS, 0, -1) for h in (d, ZG // 2 - d)]


def away(j, sizes):
    total = 0
    for size in reversed(sizes):
        total += min(j % size, size - j % size)
        j //= size
    return total


Z_ORDER = sorted(range(1, ZG), key=lambda j: -away(j // 2, (16,)))
XY_ORDER = sorted(range(1, XY), key=lambda j: -away(j, (4, 4)))


def nn(a, b):
    return lax.dot_general(a, b, (((1,), (0,)), ((), ())), preferred_element_type=F32)


def nt(a, b):
    return lax.dot_general(a, b, (((1,), (1,)), ((), ())), preferred_element_type=F32)


def iota(shape, dim):
    return lax.broadcasted_iota(I32, shape, dim)


def cut2(x):
    hi = x.astype(BF16)
    return hi, (x - hi.astype(F32)).astype(BF16)


def cut3(x):
    hi = x.astype(BF16)
    rest = x - hi.astype(F32)
    mid = rest.astype(BF16)
    return hi, mid, (rest - mid.astype(F32)).astype(BF16)


def rows3(x):
    hi = x.astype(BF16).astype(F32)
    rest = x - hi
    mid = rest.astype(BF16).astype(F32)
    low = rest - mid
    at = iota((16, x.shape[1]), 0)
    return jnp.where(at == 0, hi, jnp.where(at == 1, mid, jnp.where(at == 2, low, 0.0))).astype(BF16)


def add_rows(x):
    return jnp.sum(x, axis=0, keepdims=True)


def column(row, size):
    return jnp.sum(
        jnp.where(iota((size, size), 0) == iota((size, size), 1), row, 0.0), axis=1, keepdims=True
    )


def hot(cond):
    return jnp.where(cond, 1.0, 0.0).astype(BF16)


def build_matrix(cols, vals, mass, keep_before, keep_after, hi_ref, lo_ref):
    diag = (mass[...] + jnp.sum(jnp.abs(vals[...]), axis=0, keepdims=True)) * SCALE
    step = 64
    for block, slots in ((0, (6, 7)), (1, (0, 1, 4, 5)), (2, (2, 3))):
        for j0 in range(0, V, step):
            at = iota((step, V), 0) + (block * V + j0)
            total = jnp.zeros((step, V), F32)
            for k in slots:
                total = total + jnp.where(cols[k : k + 1, :] == at, vals[k : k + 1, :] * SCALE, 0.0)
            if block == 0:
                total = total * keep_before
            elif block == 2:
                total = total * keep_after
            else:
                total = total + jnp.where(iota((step, V), 1) == at - V, diag, 0.0)
            hi, lo = cut2(total)
            hi_ref[block * V + j0 : block * V + j0 + step, :] = hi
            lo_ref[block * V + j0 : block * V + j0 + step, :] = lo


def kernel(
    counts_h, rate_h, ri_h, pi_h, leap_h, dr_h, fw_h, ft_h, rr_h, dn_h, tt_h, tv_h, ta_h, v_h, m_h, mc_h, mv_h,
    out_h, vnew,
    counts, rate, ri, pi, leap, dr, fw, ft, rrow, dn, tt, tv, ta, v, m, mc, mv,
    xs, fire, am, ot, loc, rt, gt, ct, bh, bl, nh, nl, arr, cnew,
    slots, slots_in, pk1, rx1, nc, nv, nm, pk2, rx2, red, red_a, red_b,
    in_sem, out_sem, send_sem, recv_sem, relay_sem,
):
    me = lax.axis_index("dom")
    hbm = (counts_h, rate_h, ri_h, pi_h, leap_h, dr_h, fw_h, ft_h, rr_h, dn_h, tt_h, tv_h, ta_h, v_h, m_h, mc_h, mv_h)
    vmem = (counts, rate, ri, pi, leap, dr, fw, ft, rrow, dn, tt, tv, ta, v, m, mc, mv)
    loads = [pltpu.make_async_copy(h, d, in_sem.at[i]) for i, (h, d) in enumerate(zip(hbm, vmem))]
    for i in (7, 2, 3, 1, 0, 4, 5, 6, 9, 8, 10, 11, 12, 13, 14, 15, 16):
        loads[i].start()

    def chain(offset):
        return lax.rem(me + (offset + N), N)

    z_base = (me // ZG) * ZG
    z_at = lax.rem(me, ZG)
    xy_at = me // ZG

    def z_partner(j):
        return z_base + lax.rem(z_at + j, ZG)

    def xy_partner(j):
        return lax.rem(xy_at + j, XY) * ZG + z_at

    barrier = pltpu.get_barrier_semaphore()
    greet = [z_base + lax.rem(z_at + 2 * h, ZG) for h in NEAR_Z] + [xy_partner(j) for j in XY_ORDER]
    other_core = 1 - 2 * lax.rem(me, 2)
    greet += [z_base + lax.rem(z_at + 2 * h, ZG) + other_core for h in NEAR_Z] + [me + other_core]
    greet += [chain(o) for o in (3, -3, 2, -2, 1, -1)]
    for other in greet:
        pl.semaphore_signal(barrier, inc=1, device_id=(other,), device_id_type=MESH)

    loads[7].wait()

    def build_targets(c, carry):
        at = iota((64, T), 0) + c * 64
        start = pl.multiple_of(c * 64, 64)
        for f in range(4):
            ot[pl.ds(start, 64), f * T : (f + 1) * T] = hot(ft[f : f + 1, :] == at)
        return carry

    lax.fori_loop(0, (T + 2 * B) // 64, build_targets, 0)

    for i in (0, 1, 2, 3, 4):
        loads[i].wait()
    for i, part in enumerate(cut3(counts[...])):
        xs[i * S : (i + 1) * S, :] = part
    xs[3 * S :, :] = jnp.ones((S, T), BF16)
    lane = iota((1, 256), 1)
    wanted = jnp.where(lane < 3 * S, lax.rem(lane, S), jnp.where(lane == 3 * S, S, -1)).astype(F32)
    first = column(ri[0:1, :].astype(F32), R)
    second = column(ri[1:2, :].astype(F32), R)
    rates = column(rate[...], R)
    cap_first = jnp.where(first == S, BIG, 0.0)
    cap_second = jnp.where(second == S, BIG, 0.0)
    step = 64
    for c in range(0, R, step):
        one = first[c : c + step, :]
        two = second[c : c + step, :]
        x1 = nn(hot(one == wanted), xs[...])
        x2 = nn(hot(two == wanted), xs[...])
        prop = rates[c : c + step, :] * x1 * x2
        limit = jnp.minimum(
            jnp.maximum(x1, cap_first[c : c + step, :]), jnp.maximum(x2, cap_second[c : c + step, :])
        )
        raw = prop + jnp.sqrt(prop) * leap[c : c + step, :].astype(F32)
        hi, lo = cut2(jnp.minimum(jnp.maximum(raw, 0.0), limit))
        fire[c : c + step, :] = hi
        fire[R + c : R + c + step, :] = lo
    level = iota((S, R), 0)

    def has(row):
        return jnp.where(row == level, 1.0, 0.0)

    stoich = (has(pi[0:1, :]) + has(pi[1:2, :]) - has(ri[0:1, :]) - has(ri[1:2, :])).astype(BF16)
    delta = nn(stoich, fire[0:R, :]) + nn(stoich, fire[R:, :])
    cnew[...] = jnp.maximum(counts[...] + delta, 0.0)

    for i in (5, 6, 9):
        loads[i].wait()
    wall = T + 2 * B
    here = cnew[0:1, :]
    prob = dr[0:1, 0:1] * fw[...]
    mean = here * prob
    noise = jnp.concatenate([dn[f, 0:1, :].astype(F32) for f in range(4)], axis=0)
    raw = jnp.maximum(mean + jnp.sqrt(mean * (1.0 - prob)) * noise, 0.0)
    raw = jnp.where(ft[...] == wall, 0.0, raw)
    total = add_rows(raw)
    factor = jnp.minimum(1.0, here / jnp.maximum(total, 1.0))
    leaves = [rows3(raw[f : f + 1, :] * factor) for f in range(4)]

    def deposit(start, stop):
        out = nt(leaves[0], ot[start:stop, 0:T])
        for f in range(1, 4):
            out = out + nt(leaves[f], ot[start:stop, f * T : (f + 1) * T])
        return add_rows(out)

    out = deposit(T, T + 2 * B)
    pk1[0, :, 0:B] = out[:, 0:B]
    pk1[1, :, 0:B] = out[:, B:]
    loads[13].wait()
    for side in range(2):
        pk1[side, :, B:] = v[...]

    for i in (14, 15, 16):
        loads[i].wait()
    pl.semaphore_wait(barrier, len(greet))
    sends = []

    def send(src, dst, sem, other):
        copy = pltpu.make_async_remote_copy(
            src_ref=src, dst_ref=dst, send_sem=send_sem.at[sem], recv_sem=recv_sem.at[sem],
            device_id=(other,), device_id_type=MESH,
        )
        copy.start()
        sends.append(copy)
        return copy

    before, after = chain(-1), chain(1)
    for h in (HOPS, ZG // 2 - HOPS):
        other = z_base + lax.rem(z_at + 2 * h, ZG)
        pl.semaphore_signal(relay_sem, inc=1, device_id=(other,), device_id_type=MESH)
    small = [send(pk1.at[1], rx1.at[0], 0, after), send(pk1.at[0], rx1.at[1], 1, before)]
    params = [send(mc, nc, 2, before), send(mv, nv, 3, before), send(m, nm, 4, before)]

    first_loc = here - total * factor + deposit(0, T)
    loads[8].wait()
    loads[10].wait()
    loads[11].wait()
    loads[12].wait()
    for c in range(0, T, 64):
        at = iota((64, B), 0) + c
        rt[c : c + 64, 0:B] = hot(rrow[0:1, :] == at)
        rt[c : c + 64, B:] = hot(rrow[1:2, :] == at)
        gt[c : c + 64, :] = hot(tt[...] == iota((64, T), 0) + c)
    for c in range(0, 3 * V, 64):
        at = iota((64, T), 0) + c
        total = jnp.where(tv[0:1, :] == at, 1.0, 0.0)
        total = total + jnp.where(tv[1:2, :] == at, 1.0, 0.0)
        total = total + jnp.where(tv[2:3, :] == at, 1.0, 0.0)
        ct[c : c + 64, :] = total.astype(BF16)

    def flag(cond):
        return jnp.where(cond, 1.0, 0.0).astype(F32)

    has_before, has_after = flag(me > 0), flag(me < N - 1)
    build_matrix(mc, mv, m, has_before, has_after, bh, bl)

    def apply(x, hi_ref, lo_ref, start=0):
        parts = rows3(x)
        size = x.shape[1]
        out = nn(parts, hi_ref[start : start + size, :]) + nn(parts, lo_ref[start : start + size, :])
        return add_rows(out)

    for copy in small:
        copy.wait_recv()
    arrived = jnp.concatenate([rx1[0, :, 0:B], rx1[1, :, 0:B]], axis=1)
    c0 = first_loc + add_rows(nt(rows3(arrived), rt[...]))
    calcium = add_rows(nn(rows3(c0), gt[...]))
    share = 4.0 * ta[...] * calcium / (calcium + 2.0) / 3.0
    given = add_rows(nt(rows3(share), ct[...]))
    around = jnp.concatenate([rx1[0, :, B:], v[...], rx1[1, :, B:]], axis=1)
    start = m[...] * v[...] - apply(around, bh, bl) * (1.0 / SCALE)
    pk2[:, 0:V] = start + given[:, V : 2 * V]
    pk2[:, V : 2 * V] = given[:, 0:V]
    pk2[:, 2 * V :] = given[:, 2 * V :]

    parts2 = [send(pk2, rx2.at[i], 7 + i, chain(-o)) for i, o in enumerate((-2, -1, 1, 2, 3))]

    for copy in params:
        copy.wait_recv()
    build_matrix(nc, nv, nm, 1.0, flag(me < N - 2), nh, nl)
    hop = column(dr[...], S)
    step = 16
    for c in range(0, S, step):
        here = cnew[c : c + step, :]
        raws = []
        for f in range(4):
            prob = hop[c : c + step, :] * fw[f : f + 1, :]
            mean = here * prob
            spread = jnp.sqrt(mean * (1.0 - prob))
            raw = jnp.maximum(mean + spread * dn[f, c : c + step, :].astype(F32), 0.0)
            raws.append(jnp.where(ft[f : f + 1, :] == wall, 0.0, raw))
        total = raws[0] + raws[1] + raws[2] + raws[3]
        factor = jnp.minimum(1.0, here / jnp.maximum(total, 1.0))
        for f in range(4):
            hi, lo = cut2(raws[f] * factor)
            am[c : c + step, f * T : (f + 1) * T] = hi
            am[S + c : S + c + step, f * T : (f + 1) * T] = lo
        loc[c : c + step, :] = here - total * factor
    for side in range(2):
        out = nt(am[...], ot[T + side * B : T + (side + 1) * B, :])
        slots[side] = out[:S, :] + out[S:, :]
    bulk = [send(slots.at[1], slots_in.at[0], 5, after), send(slots.at[0], slots_in.at[1], 6, before)]
    for w in range(0, T, 256):
        out = nt(am[...], ot[w : w + 256, :])
        loc[:, w : w + 256] = loc[:, w : w + 256] + out[:S, :] + out[S:, :]
    for copy in parts2:
        copy.wait_recv()
    own_e, own_b, own_a = pk2[:, 0:V], pk2[:, V : 2 * V], pk2[:, 2 * V :]
    r_own = own_e + rx2[1, :, 2 * V :] + rx2[2, :, V : 2 * V]
    r_before = rx2[1, :, 0:V] + own_b + rx2[0, :, 2 * V :]
    r_after = rx2[2, :, 0:V] + own_a + rx2[3, :, V : 2 * V]
    r_after2 = rx2[3, :, 0:V] + rx2[2, :, 2 * V :] + rx2[4, :, V : 2 * V]
    u_own = apply(jnp.concatenate([r_before, r_own, r_after], axis=1), bh, bl)
    u_after = apply(jnp.concatenate([r_own, r_after, r_after2], axis=1), nh, nl)
    t_own = apply(jnp.concatenate([u_own, 2.0 * u_after], axis=1), bh, bl, V)

    def fold(x):
        return x[:, 0:128] + x[:, 128:256]

    products = (fold(r_own * r_own), fold(r_own * u_own), fold(u_own * u_own), fold(u_own * t_own))
    at = iota((8, 128), 0)
    stack = jnp.zeros((8, 128), F32)
    for i, p in enumerate(products):
        stack = jnp.where(at == i, p, stack)
    sums = jnp.sum(stack, axis=1, keepdims=True)
    red[0] = add_rows(jnp.where(at == iota((8, 128), 1), sums, 0.0))

    def reduce(stage, partner, order, buffer, sem):
        for j in order:
            pltpu.make_async_remote_copy(
                src_ref=red.at[stage], dst_ref=buffer.at[j - 1], send_sem=send_sem.at[sem],
                recv_sem=recv_sem.at[sem], device_id=(partner(j),), device_id_type=MESH,
            ).start()

    pl.semaphore_wait(relay_sem, 2)
    reduce(0, z_partner, Z_ORDER, red_a, 12)

    for copy in bulk:
        copy.wait_recv()
    for side in range(2):
        hi, lo = cut2(slots_in[side])
        arr[0:S, side * B : (side + 1) * B] = hi
        arr[S:, side * B : (side + 1) * B] = lo
    for w in range(0, T, 256):
        out = nt(arr[...], rt[w : w + 256, :])
        cnew[:, w : w + 256] = loc[:, w : w + 256] + out[:S, :] + out[S:, :]

    out_copy = pltpu.make_async_copy(cnew, out_h, out_sem)
    out_copy.start()

    pltpu.make_async_copy(red_a, red_a, recv_sem.at[12]).wait()
    red[1] = red[0] + jnp.sum(red_a[...], axis=0)
    reduce(1, xy_partner, XY_ORDER, red_b, 13)
    pltpu.make_async_copy(red_b, red_b, recv_sem.at[13]).wait()
    final = red[1] + jnp.sum(red_b[...], axis=0)
    rr, ru, uu, ut = (final[:, i : i + 1] for i in range(4))
    alpha0 = rr / ru
    norm1 = alpha0 * alpha0 * uu - rr
    keep = 1.0 + norm1 / rr
    curve = keep * keep * ru - 2.0 * keep * alpha0 * uu + alpha0 * alpha0 * ut
    alpha1 = norm1 / curve
    direction = keep * r_own - alpha0 * u_own
    vnew[...] = v[...] + (alpha0 * SCALE) * r_own + (alpha1 * SCALE) * direction
    for copy in sends:
        copy.wait_send()
    pltpu.make_async_copy(red_a, red_a, send_sem.at[12]).wait()
    pltpu.make_async_copy(red_b, red_b, send_sem.at[13]).wait()
    out_copy.wait()


def finish(counts_in, v_in, counts_out, v_out, hold, hold_v, in_sem, out_sem):
    rows = S // PIECES
    parts = [slice(i * rows, (i + 1) * rows) for i in range(PIECES)]
    loads = [pltpu.make_async_copy(v_in, hold_v, in_sem.at[PIECES])]
    stores = [pltpu.make_async_copy(hold_v, v_out, out_sem.at[PIECES])]
    for i, part in enumerate(parts):
        loads.append(pltpu.make_async_copy(counts_in.at[part, :], hold.at[part, :], in_sem.at[i]))
        stores.append(pltpu.make_async_copy(hold.at[part, :], counts_out.at[part, :], out_sem.at[i]))
    for copy in loads:
        copy.start()
    for load, store in zip(loads, stores):
        load.wait()
        store.start()
    for copy in stores:
        copy.wait()


def per_device(*args):
    shaped = [a.reshape(1, -1) if a.ndim == 1 else a for a in args]
    any_spec = pl.BlockSpec(memory_space=pl.ANY)
    scratch = [pltpu.VMEM(a.shape, a.dtype) for a in shaped]
    scratch += [
        pltpu.VMEM((256, T), BF16),
        pltpu.VMEM((2 * R, T), BF16),
        pltpu.VMEM((2 * S, 4 * T), BF16),
        pltpu.VMEM((T + 2 * B, 4 * T), BF16),
        pltpu.VMEM((S, T), F32),
        pltpu.VMEM((T, 2 * B), BF16),
        pltpu.VMEM((T, T), BF16),
        pltpu.VMEM((3 * V, T), BF16),
        pltpu.VMEM((3 * V, V), BF16),
        pltpu.VMEM((3 * V, V), BF16),
        pltpu.VMEM((3 * V, V), BF16),
        pltpu.VMEM((3 * V, V), BF16),
        pltpu.VMEM((2 * S, 2 * B), BF16),
        pltpu.VMEM((S, T), F32),
        pltpu.VMEM((2, S, B), F32),
        pltpu.VMEM((2, S, B), F32),
        pltpu.VMEM((2, 1, B + V), F32),
        pltpu.VMEM((2, 1, B + V), F32),
        pltpu.VMEM((8, V), I32),
        pltpu.VMEM((8, V), F32),
        pltpu.VMEM((1, V), F32),
        pltpu.VMEM((1, 3 * V), F32),
        pltpu.VMEM((5, 1, 3 * V), F32),
        pltpu.VMEM((2, 1, 128), F32),
        pltpu.VMEM((ZG - 1, 1, 128), F32),
        pltpu.VMEM((XY - 1, 1, 128), F32),
        pltpu.SemaphoreType.DMA((17,)),
        pltpu.SemaphoreType.DMA,
        pltpu.SemaphoreType.DMA((14,)),
        pltpu.SemaphoreType.DMA((14,)),
        pltpu.SemaphoreType.REGULAR,
    ]
    counts_new, voltage = pl.pallas_call(
        kernel,
        name="step",
        out_shape=(jax.ShapeDtypeStruct((S, T), F32), jax.ShapeDtypeStruct((1, V), F32)),
        in_specs=[any_spec] * len(shaped),
        out_specs=(any_spec, pl.BlockSpec(memory_space=pltpu.VMEM)),
        scratch_shapes=scratch,
        compiler_params=pltpu.CompilerParams(
            collective_id=1, has_side_effects=True, vmem_limit_bytes=60 * 1024 * 1024
        ),
    )(*shaped)
    counts_new, voltage = pl.pallas_call(
        finish,
        name="finish",
        out_shape=(jax.ShapeDtypeStruct((S, T), F32), jax.ShapeDtypeStruct((1, V), F32)),
        in_specs=[any_spec, any_spec],
        out_specs=(any_spec, any_spec),
        scratch_shapes=[
            pltpu.VMEM((S, T), F32),
            pltpu.VMEM((1, V), F32),
            pltpu.SemaphoreType.DMA((PIECES + 1,)),
            pltpu.SemaphoreType.DMA((PIECES + 1,)),
        ],
        compiler_params=pltpu.CompilerParams(vmem_limit_bytes=60 * 1024 * 1024),
    )(counts_new, voltage)
    return counts_new, voltage.reshape(-1)


def solution(mesh):
    placed = (
        P(None, "dom"), P(), P(), P(), P(None, "dom"), P(), P(None, "dom"), P(None, "dom"), P(None, "dom"),
        P(None, None, "dom"), P("dom"), P(None, "dom"), P("dom"), P("dom"), P("dom"), P(None, "dom"),
        P(None, "dom"),
    )
    return jax.shard_map(
        per_device, mesh=mesh, in_specs=placed, out_specs=(P(None, "dom"), P("dom")), check_vma=False
    )
```

```python
import jax
import jax.numpy as jnp
from jax import lax
from jax.experimental import pallas as pl
from jax.experimental.pallas import tpu as pltpu
from jax.sharding import PartitionSpec as P

F32 = jnp.float32
BF16 = jnp.bfloat16
I32 = jnp.int32
MESH = pl.DeviceIdType.MESH

N = 512
S = 64
R = 256
T = 512
B = 256
V = 256
BIG = 1e30
SCALE = 1.0 / 32.0
ZG = 32
XY = 16


HOPS = 2
XY_SIDE = 4
PIECES = 2
NEAR_Z = [h for d in range(HOPS, 0, -1) for h in (d, ZG // 2 - d)]


def away(j, sizes):
    total = 0
    for size in reversed(sizes):
        total += min(j % size, size - j % size)
        j //= size
    return total


Z_ORDER = sorted(range(1, ZG), key=lambda j: -away(j // 2, (16,)))
XY_ORDER = sorted(range(1, XY), key=lambda j: -away(j, (XY_SIDE, XY_SIDE)))
NEAR_XY = [j for j in XY_ORDER if away(j, (XY_SIDE, XY_SIDE)) <= HOPS]
XY_MIDDLE = (2 * XY_SIDE, 2)


def nn(a, b):
    return lax.dot_general(a, b, (((1,), (0,)), ((), ())), preferred_element_type=F32)


def nt(a, b):
    return lax.dot_general(a, b, (((1,), (1,)), ((), ())), preferred_element_type=F32)


def iota(shape, dim):
    return lax.broadcasted_iota(I32, shape, dim)


def cut2(x):
    hi = x.astype(BF16)
    return hi, (x - hi.astype(F32)).astype(BF16)


def cut3(x):
    hi = x.astype(BF16)
    rest = x - hi.astype(F32)
    mid = rest.astype(BF16)
    return hi, mid, (rest - mid.astype(F32)).astype(BF16)


def rows3(x):
    hi = x.astype(BF16).astype(F32)
    rest = x - hi
    mid = rest.astype(BF16).astype(F32)
    low = rest - mid
    at = iota((16, x.shape[1]), 0)
    return jnp.where(at == 0, hi, jnp.where(at == 1, mid, jnp.where(at == 2, low, 0.0))).astype(BF16)


def add_rows(x):
    return jnp.sum(x, axis=0, keepdims=True)


def column(row):
    size = min(row.shape[1], 128)
    same = iota((size, size), 0) == iota((size, size), 1)
    blocks = [
        jnp.sum(jnp.where(same, row[:, at : at + size], 0.0), axis=1, keepdims=True)
        for at in range(0, row.shape[1], size)
    ]
    return blocks[0] if len(blocks) == 1 else jnp.concatenate(blocks, axis=0)


def split3(x):
    hi = x.astype(BF16).astype(F32)
    rest = x - hi
    mid = rest.astype(BF16).astype(F32)
    return hi, mid, rest - mid


def by_block(x, index):
    at = (index >> 7) == iota((8, x.shape[1]), 0)
    parts = [jnp.where(at, part, 0.0) for part in split3(x)]
    return jnp.concatenate(parts + [jnp.zeros((8, x.shape[1]), F32)], axis=0).astype(BF16)


def low_hot(index):
    return hot((index & 127) == iota((128, index.shape[1]), 0))


def groups(x):
    return x[0:8, :] + x[8:16, :] + x[16:24, :]


def hot(cond):
    return jnp.where(cond, 1.0, 0.0).astype(BF16)


def build_matrix(cols, vals, mass, keep_before, keep_after, hi_ref, lo_ref):
    diag = (mass[...] + jnp.sum(jnp.abs(vals[...]), axis=0, keepdims=True)) * SCALE
    step = 64
    for block, slots in ((0, (6, 7)), (1, (0, 1, 4, 5)), (2, (2, 3))):
        for j0 in range(0, V, step):
            at = iota((step, V), 0) + (block * V + j0)
            total = jnp.zeros((step, V), F32)
            for k in slots:
                total = total + jnp.where(cols[k : k + 1, :] == at, vals[k : k + 1, :] * SCALE, 0.0)
            if block == 0:
                total = total * keep_before
            elif block == 2:
                total = total * keep_after
            else:
                total = total + jnp.where(iota((step, V), 1) == at - V, diag, 0.0)
            hi, lo = cut2(total)
            hi_ref[block * V + j0 : block * V + j0 + step, :] = hi
            lo_ref[block * V + j0 : block * V + j0 + step, :] = lo


def kernel(
    counts_h, rate_h, ri_h, pi_h, leap_h, dr_h, fw_h, ft_h, rr_h, dn_h, tt_h, tv_h, ta_h, v_h, m_h, mc_h, mv_h,
    out_h, vnew,
    counts, rate, ri, pi, leap, dr, fw, ft, rrow, dn, tt, tv, ta, v, m, mc, mv,
    xs, sel, fire, am, ot, loc, rt, fb, rb, tb, vb, bh, bl, nh, nl, arr, cnew,
    slots, slots_in, pk1, rx1, nc, nv, nm, pk2, rx2, red, red_a, red_b,
    in_sem, out_sem, send_sem, recv_sem, relay_sem,
):
    me = lax.axis_index("dom")
    hbm = (counts_h, rate_h, ri_h, pi_h, leap_h, dr_h, fw_h, ft_h, rr_h, dn_h, tt_h, tv_h, ta_h, v_h, m_h, mc_h, mv_h)
    vmem = (counts, rate, ri, pi, leap, dr, fw, ft, rrow, dn, tt, tv, ta, v, m, mc, mv)
    loads = [pltpu.make_async_copy(h, d, in_sem.at[i]) for i, (h, d) in enumerate(zip(hbm, vmem))]
    for i in (7, 2, 3, 1, 0, 4, 5, 6, 9, 8, 10, 11, 12, 13, 14, 15, 16):
        loads[i].start()

    def chain(offset):
        return lax.rem(me + (offset + N), N)

    z_base = (me // ZG) * ZG
    z_at = lax.rem(me, ZG)
    xy_at = me // ZG

    def z_partner(j):
        return z_base + lax.rem(z_at + j, ZG)

    def xy_partner(j):
        x = lax.rem(xy_at // XY_SIDE + j // XY_SIDE, XY_SIDE)
        y = lax.rem(lax.rem(xy_at, XY_SIDE) + j % XY_SIDE, XY_SIDE)
        return (x * XY_SIDE + y) * ZG + z_at

    def z_chip(h):
        return z_base + lax.rem(z_at + 2 * h, ZG)

    barrier = pltpu.get_barrier_semaphore()
    other_core = 1 - 2 * lax.rem(me, 2)
    greet = [chain(o) for o in (3, -3, 2, -2, 1, -1)] + [xy_partner(j) for j in NEAR_XY]
    greet += [z_chip(h) for h in NEAR_Z] + [z_chip(h) + other_core for h in NEAR_Z] + [me + other_core]
    for other in greet:
        pl.semaphore_signal(barrier, inc=1, device_id=(other,), device_id_type=MESH)

    loads[7].wait()

    for f in range(4):
        fb[:, f * T : (f + 1) * T] = low_hot(ft[f : f + 1, :])

    for i in (1, 2, 3):
        loads[i].wait()
    lane = iota((1, 256), 1)
    wanted = jnp.where(lane < 3 * S, lax.rem(lane, S), jnp.where(lane == 3 * S, S, -1)).astype(F32)
    first = column(ri[0:1, :].astype(F32))
    second = column(ri[1:2, :].astype(F32))
    rates = column(rate[...])
    sel[:, 0:256] = hot(first == wanted)
    sel[:, 256:] = hot(second == wanted)
    cap_first = jnp.where(first == S, BIG, 0.0)
    cap_second = jnp.where(second == S, BIG, 0.0)
    level = iota((S, R), 0)

    def has(row):
        return jnp.where(row == level, 1.0, 0.0)

    stoich = (has(pi[0:1, :]) + has(pi[1:2, :]) - has(ri[0:1, :]) - has(ri[1:2, :])).astype(BF16)
    loads[0].wait()
    for i, part in enumerate(cut3(counts[...])):
        xs[i * S : (i + 1) * S, :] = part
    xs[3 * S :, :] = jnp.ones((S, T), BF16)
    loads[4].wait()
    step = 64
    for c in range(0, R, step):
        x1 = nn(sel[c : c + step, 0:256], xs[...])
        x2 = nn(sel[c : c + step, 256:], xs[...])
        prop = rates[c : c + step, :] * x1 * x2
        limit = jnp.minimum(
            jnp.maximum(x1, cap_first[c : c + step, :]), jnp.maximum(x2, cap_second[c : c + step, :])
        )
        raw = prop + jnp.sqrt(prop) * leap[c : c + step, :].astype(F32)
        hi, lo = cut2(jnp.minimum(jnp.maximum(raw, 0.0), limit))
        fire[c : c + step, :] = hi
        fire[R + c : R + c + step, :] = lo
    delta = nn(stoich, fire[0:R, :]) + nn(stoich, fire[R:, :])
    cnew[...] = jnp.maximum(counts[...] + delta, 0.0)

    for i in (5, 6, 9):
        loads[i].wait()
    wall = T + 2 * B
    here = cnew[0:1, :]
    prob = dr[0:1, 0:1] * fw[...]
    mean = here * prob
    noise = jnp.concatenate([dn[f, 0:1, :].astype(F32) for f in range(4)], axis=0)
    raw = jnp.maximum(mean + jnp.sqrt(mean * (1.0 - prob)) * noise, 0.0)
    raw = jnp.where(ft[...] == wall, 0.0, raw)
    total = add_rows(raw)
    factor = jnp.minimum(1.0, here / jnp.maximum(total, 1.0))
    stays = here - total * factor
    leaves = [by_block(raw[f : f + 1, :] * factor, ft[f : f + 1, :]) for f in range(4)]
    out = groups(nt(jnp.concatenate(leaves, axis=1), fb[...]))
    own = out + jnp.concatenate([stays[:, a * 128 : (a + 1) * 128] for a in range(4)] * 2, axis=0)
    for side in range(2):
        for a in range(2):
            row = T // 128 + 2 * side + a
            pk1[side, :, a * 128 : (a + 1) * 128] = out[row : row + 1, :]
    loads[13].wait()
    for side in range(2):
        pk1[side, :, B:] = v[...]

    for i in (14, 15, 16):
        loads[i].wait()
    pl.semaphore_wait(barrier, len(greet))
    sends = []

    def send(src, dst, sem, other):
        copy = pltpu.make_async_remote_copy(
            src_ref=src, dst_ref=dst, send_sem=send_sem.at[sem], recv_sem=recv_sem.at[sem],
            device_id=(other,), device_id_type=MESH,
        )
        copy.start()
        sends.append(copy)
        return copy

    before, after = chain(-1), chain(1)
    def relay(others, level):
        for other in others:
            pl.semaphore_signal(relay_sem.at[level], inc=1, device_id=(other,), device_id_type=MESH)

    small = [send(pk1.at[1], rx1.at[0], 0, after), send(pk1.at[0], rx1.at[1], 1, before)]
    relay([z_chip(HOPS), z_chip(ZG // 2 - HOPS)], 0)
    relay([xy_partner(j) for j in XY_MIDDLE], 1)
    params = [send(mc, nc, 2, before), send(mv, nv, 3, before), send(m, nm, 4, before)]

    for i in (8, 10, 11, 12):
        loads[i].wait()
    recv = jnp.concatenate([rrow[0:1, :], rrow[1:2, :]], axis=1)
    rb[...] = low_hot(recv)
    tb[...] = low_hot(tt[...])
    for c in range(3):
        vb[:, c * T : (c + 1) * T] = low_hot(tv[c : c + 1, :])

    def flag(cond):
        return jnp.where(cond, 1.0, 0.0).astype(F32)

    has_before, has_after = flag(me > 0), flag(me < N - 1)
    build_matrix(mc, mv, m, has_before, has_after, bh, bl)

    def build_targets(c, carry):
        at = iota((64, T), 0) + c * 64
        start = pl.multiple_of(c * 64, 64)
        for f in range(4):
            ot[pl.ds(start, 64), f * T : (f + 1) * T] = hot(ft[f : f + 1, :] == at)
        return carry

    lax.fori_loop(0, (T + 2 * B) // 64, build_targets, 0)

    def apply(x, hi_ref, lo_ref, start=0):
        parts = rows3(x)
        size = x.shape[1]
        out = nn(parts, hi_ref[start : start + size, :]) + nn(parts, lo_ref[start : start + size, :])
        return add_rows(out)

    for copy in small:
        copy.wait_recv()
    arrived = jnp.concatenate([rx1[0, :, 0:B], rx1[1, :, 0:B]], axis=1)
    c0 = own + groups(nt(by_block(arrived, recv), rb[...]))
    parts = jnp.concatenate(split3(c0) + (jnp.zeros((8, 128), F32),), axis=0).astype(BF16)
    picked = groups(nn(parts, tb[...]))
    calcium = add_rows(jnp.where((tt[...] >> 7) == iota((8, T), 0), picked, 0.0))
    share = 4.0 * ta[...] * calcium / (calcium + 2.0) / 3.0
    corners = jnp.concatenate([by_block(share, tv[c : c + 1, :]) for c in range(3)], axis=1)
    given = groups(nt(corners, vb[...]))
    around = jnp.concatenate([rx1[0, :, B:], v[...], rx1[1, :, B:]], axis=1)
    start = m[...] * v[...] - apply(around, bh, bl) * (1.0 / SCALE)
    for a in range(2):
        half = slice(a * 128, (a + 1) * 128)
        pk2[:, half] = start[:, half] + given[2 + a : 3 + a, :]
        pk2[:, V + a * 128 : V + (a + 1) * 128] = given[a : a + 1, :]
        pk2[:, 2 * V + a * 128 : 2 * V + (a + 1) * 128] = given[4 + a : 5 + a, :]

    parts2 = [send(pk2, rx2.at[i], 7 + i, chain(-o)) for i, o in enumerate((-2, -1, 1, 2, 3))]

    pl.semaphore_wait(relay_sem.at[0], 2)
    relay([z_chip(2 * HOPS), z_chip(ZG // 2 - 2 * HOPS)], 2)
    for copy in params:
        copy.wait_recv()
    build_matrix(nc, nv, nm, 1.0, flag(me < N - 2), nh, nl)
    for copy in parts2:
        copy.wait_recv()
    own_e, own_b, own_a = pk2[:, 0:V], pk2[:, V : 2 * V], pk2[:, 2 * V :]
    r_own = own_e + rx2[1, :, 2 * V :] + rx2[2, :, V : 2 * V]
    r_before = rx2[1, :, 0:V] + own_b + rx2[0, :, 2 * V :]
    r_after = rx2[2, :, 0:V] + own_a + rx2[3, :, V : 2 * V]
    r_after2 = rx2[3, :, 0:V] + rx2[2, :, 2 * V :] + rx2[4, :, V : 2 * V]
    u_own = apply(jnp.concatenate([r_before, r_own, r_after], axis=1), bh, bl)
    u_after = apply(jnp.concatenate([r_own, r_after, r_after2], axis=1), nh, nl)
    t_own = apply(jnp.concatenate([u_own, 2.0 * u_after], axis=1), bh, bl, V)

    def fold(x):
        return x[:, 0:128] + x[:, 128:256]

    products = (fold(r_own * r_own), fold(r_own * u_own), fold(u_own * u_own), fold(u_own * t_own))
    at = iota((8, 128), 0)
    stack = jnp.zeros((8, 128), F32)
    for i, p in enumerate(products):
        stack = jnp.where(at == i, p, stack)
    sums = jnp.sum(stack, axis=1, keepdims=True)
    red[0] = add_rows(jnp.where(at == iota((8, 128), 1), sums, 0.0))

    def reduce(stage, partner, order, buffer, sem):
        for j in order:
            pltpu.make_async_remote_copy(
                src_ref=red.at[stage], dst_ref=buffer.at[j - 1], send_sem=send_sem.at[sem],
                recv_sem=recv_sem.at[sem], device_id=(partner(j),), device_id_type=MESH,
            ).start()

    pl.semaphore_wait(relay_sem.at[2], 2)
    reduce(0, z_partner, Z_ORDER, red_a, 12)


    hop = column(dr[...])
    step = 16
    for c in range(0, S, step):
        here = cnew[c : c + step, :]
        raws = []
        for f in range(4):
            prob = hop[c : c + step, :] * fw[f : f + 1, :]
            mean = here * prob
            spread = jnp.sqrt(mean * (1.0 - prob))
            raw = jnp.maximum(mean + spread * dn[f, c : c + step, :].astype(F32), 0.0)
            raws.append(jnp.where(ft[f : f + 1, :] == wall, 0.0, raw))
        total = raws[0] + raws[1] + raws[2] + raws[3]
        factor = jnp.minimum(1.0, here / jnp.maximum(total, 1.0))
        for f in range(4):
            hi, lo = cut2(raws[f] * factor)
            am[c : c + step, f * T : (f + 1) * T] = hi
            am[S + c : S + c + step, f * T : (f + 1) * T] = lo
        loc[c : c + step, :] = here - total * factor
    for side in range(2):
        out = nt(ot[T + side * B : T + (side + 1) * B, :], am[...]).T
        slots[side] = out[:S, :] + out[S:, :]
    bulk = [send(slots.at[1], slots_in.at[0], 5, after), send(slots.at[0], slots_in.at[1], 6, before)]
    for w in range(0, T, 256):
        out = nt(ot[w : w + 256, :], am[...]).T
        loc[:, w : w + 256] = loc[:, w : w + 256] + out[:S, :] + out[S:, :]
    for c in range(0, T, 64):
        at = iota((64, B), 0) + c
        rt[c : c + 64, 0:B] = hot(rrow[0:1, :] == at)
        rt[c : c + 64, B:] = hot(rrow[1:2, :] == at)

    pltpu.make_async_copy(red_a, red_a, recv_sem.at[12]).wait()
    red[1] = red[0] + jnp.sum(red_a[...], axis=0)
    pl.semaphore_wait(relay_sem.at[1], 2)
    reduce(1, xy_partner, XY_ORDER, red_b, 13)

    for copy in bulk:
        copy.wait_recv()
    for side in range(2):
        hi, lo = cut2(slots_in[side])
        arr[0:S, side * B : (side + 1) * B] = hi
        arr[S:, side * B : (side + 1) * B] = lo
    for w in range(0, T, 256):
        out = nt(rt[w : w + 256, :], arr[...]).T
        cnew[:, w : w + 256] = loc[:, w : w + 256] + out[:S, :] + out[S:, :]

    out_copy = pltpu.make_async_copy(cnew, out_h, out_sem)
    out_copy.start()

    pltpu.make_async_copy(red_b, red_b, recv_sem.at[13]).wait()
    final = red[1] + jnp.sum(red_b[...], axis=0)
    rr, ru, uu, ut = (final[:, i : i + 1] for i in range(4))
    alpha0 = rr / ru
    norm1 = alpha0 * alpha0 * uu - rr
    keep = 1.0 + norm1 / rr
    curve = keep * keep * ru - 2.0 * keep * alpha0 * uu + alpha0 * alpha0 * ut
    alpha1 = norm1 / curve
    direction = keep * r_own - alpha0 * u_own
    vnew[...] = v[...] + (alpha0 * SCALE) * r_own + (alpha1 * SCALE) * direction
    for copy in sends:
        copy.wait_send()
    pltpu.make_async_copy(red_a, red_a, send_sem.at[12]).wait()
    pltpu.make_async_copy(red_b, red_b, send_sem.at[13]).wait()
    out_copy.wait()


def finish(counts_in, v_in, counts_out, v_out, hold, hold_v, in_sem, out_sem):
    rows = S // PIECES
    parts = [slice(i * rows, (i + 1) * rows) for i in range(PIECES)]
    loads = [pltpu.make_async_copy(v_in, hold_v, in_sem.at[PIECES])]
    stores = [pltpu.make_async_copy(hold_v, v_out, out_sem.at[PIECES])]
    for i, part in enumerate(parts):
        loads.append(pltpu.make_async_copy(counts_in.at[part, :], hold.at[part, :], in_sem.at[i]))
        stores.append(pltpu.make_async_copy(hold.at[part, :], counts_out.at[part, :], out_sem.at[i]))
    for copy in loads:
        copy.start()
    for load, store in zip(loads, stores):
        load.wait()
        store.start()
    for copy in stores:
        copy.wait()


def per_device(*args):
    shaped = [a.reshape(1, -1) if a.ndim == 1 else a for a in args]
    any_spec = pl.BlockSpec(memory_space=pl.ANY)
    scratch = [pltpu.VMEM(a.shape, a.dtype) for a in shaped]
    scratch += [
        pltpu.VMEM((256, T), BF16),
        pltpu.VMEM((R, 512), BF16),
        pltpu.VMEM((2 * R, T), BF16),
        pltpu.VMEM((2 * S, 4 * T), BF16),
        pltpu.VMEM((T + 2 * B, 4 * T), BF16),
        pltpu.VMEM((S, T), F32),
        pltpu.VMEM((T, 2 * B), BF16),
        pltpu.VMEM((128, 4 * T), BF16),
        pltpu.VMEM((128, 2 * B), BF16),
        pltpu.VMEM((128, T), BF16),
        pltpu.VMEM((128, 3 * T), BF16),
        pltpu.VMEM((3 * V, V), BF16),
        pltpu.VMEM((3 * V, V), BF16),
        pltpu.VMEM((3 * V, V), BF16),
        pltpu.VMEM((3 * V, V), BF16),
        pltpu.VMEM((2 * S, 2 * B), BF16),
        pltpu.VMEM((S, T), F32),
        pltpu.VMEM((2, S, B), F32),
        pltpu.VMEM((2, S, B), F32),
        pltpu.VMEM((2, 1, B + V), F32),
        pltpu.VMEM((2, 1, B + V), F32),
        pltpu.VMEM((8, V), I32),
        pltpu.VMEM((8, V), F32),
        pltpu.VMEM((1, V), F32),
        pltpu.VMEM((1, 3 * V), F32),
        pltpu.VMEM((5, 1, 3 * V), F32),
        pltpu.VMEM((2, 1, 128), F32),
        pltpu.VMEM((ZG - 1, 1, 128), F32),
        pltpu.VMEM((XY - 1, 1, 128), F32),
        pltpu.SemaphoreType.DMA((17,)),
        pltpu.SemaphoreType.DMA,
        pltpu.SemaphoreType.DMA((14,)),
        pltpu.SemaphoreType.DMA((14,)),
        pltpu.SemaphoreType.REGULAR((3,)),
    ]
    counts_new, voltage = pl.pallas_call(
        kernel,
        name="step",
        out_shape=(jax.ShapeDtypeStruct((S, T), F32), jax.ShapeDtypeStruct((1, V), F32)),
        in_specs=[any_spec] * len(shaped),
        out_specs=(any_spec, pl.BlockSpec(memory_space=pltpu.VMEM)),
        scratch_shapes=scratch,
        compiler_params=pltpu.CompilerParams(
            collective_id=1, has_side_effects=True, vmem_limit_bytes=60 * 1024 * 1024
        ),
    )(*shaped)
    counts_new, voltage = pl.pallas_call(
        finish,
        name="finish",
        out_shape=(jax.ShapeDtypeStruct((S, T), F32), jax.ShapeDtypeStruct((1, V), F32)),
        in_specs=[any_spec, any_spec],
        out_specs=(any_spec, any_spec),
        scratch_shapes=[
            pltpu.VMEM((S, T), F32),
            pltpu.VMEM((1, V), F32),
            pltpu.SemaphoreType.DMA((PIECES + 1,)),
            pltpu.SemaphoreType.DMA((PIECES + 1,)),
        ],
        compiler_params=pltpu.CompilerParams(vmem_limit_bytes=60 * 1024 * 1024),
    )(counts_new, voltage)
    return counts_new, voltage.reshape(-1)


def solution(mesh):
    placed = (
        P(None, "dom"), P(), P(), P(), P(None, "dom"), P(), P(None, "dom"), P(None, "dom"), P(None, "dom"),
        P(None, None, "dom"), P("dom"), P(None, "dom"), P("dom"), P("dom"), P("dom"), P(None, "dom"),
        P(None, "dom"),
    )
    return jax.shard_map(
        per_device, mesh=mesh, in_specs=placed, out_specs=(P(None, "dom"), P("dom")), check_vma=False
    )
```

```python
import jax
import jax.numpy as jnp
from jax import lax
from jax.experimental import pallas as pl
from jax.experimental.pallas import tpu as pltpu
from jax.sharding import PartitionSpec as P

F32 = jnp.float32
BF16 = jnp.bfloat16
I32 = jnp.int32
MESH = pl.DeviceIdType.MESH

N = 512
S = 64
R = 256
T = 512
B = 256
V = 256
BIG = 1e30
SCALE = 1.0 / 32.0
ZG = 32
XY = 16


HOPS = 2
XY_SIDE = 4
PIECES = 2
NEAR_Z = [h for d in range(HOPS, 0, -1) for h in (d, ZG // 2 - d)]


def away(j, sizes):
    total = 0
    for size in reversed(sizes):
        total += min(j % size, size - j % size)
        j //= size
    return total


Z_ORDER = sorted(range(1, ZG), key=lambda j: -away(j // 2, (16,)))
XY_ORDER = sorted(range(1, XY), key=lambda j: -away(j, (XY_SIDE, XY_SIDE)))
NEAR_XY = [j for j in XY_ORDER if away(j, (XY_SIDE, XY_SIDE)) <= HOPS]
XY_MIDDLE = (2 * XY_SIDE, 2)


def nn(a, b):
    return lax.dot_general(a, b, (((1,), (0,)), ((), ())), preferred_element_type=F32)


def nt(a, b):
    return lax.dot_general(a, b, (((1,), (1,)), ((), ())), preferred_element_type=F32)


def iota(shape, dim):
    return lax.broadcasted_iota(I32, shape, dim)


def cut2(x):
    hi = x.astype(BF16)
    return hi, (x - hi.astype(F32)).astype(BF16)


def cut3(x):
    hi = x.astype(BF16)
    rest = x - hi.astype(F32)
    mid = rest.astype(BF16)
    return hi, mid, (rest - mid.astype(F32)).astype(BF16)


def rows3(x):
    hi = x.astype(BF16).astype(F32)
    rest = x - hi
    mid = rest.astype(BF16).astype(F32)
    low = rest - mid
    at = iota((16, x.shape[1]), 0)
    return jnp.where(at == 0, hi, jnp.where(at == 1, mid, jnp.where(at == 2, low, 0.0))).astype(BF16)


def add_rows(x):
    return jnp.sum(x, axis=0, keepdims=True)


def column(row):
    size = min(row.shape[1], 128)
    same = iota((size, size), 0) == iota((size, size), 1)
    blocks = [
        jnp.sum(jnp.where(same, row[:, at : at + size], 0.0), axis=1, keepdims=True)
        for at in range(0, row.shape[1], size)
    ]
    return blocks[0] if len(blocks) == 1 else jnp.concatenate(blocks, axis=0)


def split3(x):
    hi = x.astype(BF16).astype(F32)
    rest = x - hi
    mid = rest.astype(BF16).astype(F32)
    return hi, mid, rest - mid


def by_block(x, index):
    at = (index >> 7) == iota((8, x.shape[1]), 0)
    parts = [jnp.where(at, part, 0.0) for part in split3(x)]
    return jnp.concatenate(parts + [jnp.zeros((8, x.shape[1]), F32)], axis=0).astype(BF16)


def low_hot(index):
    return hot((index & 127) == iota((128, index.shape[1]), 0))


def groups(x):
    return x[0:8, :] + x[8:16, :] + x[16:24, :]


def hot(cond):
    return jnp.where(cond, 1.0, 0.0).astype(BF16)


def build_matrix(cols, vals, mass, keep_before, keep_after, hi_ref, lo_ref):
    diag = (mass[...] + jnp.sum(jnp.abs(vals[...]), axis=0, keepdims=True)) * SCALE
    step = 64
    for block, slots in ((0, (6, 7)), (1, (0, 1, 4, 5)), (2, (2, 3))):
        for j0 in range(0, V, step):
            at = iota((step, V), 0) + (block * V + j0)
            total = jnp.zeros((step, V), F32)
            for k in slots:
                total = total + jnp.where(cols[k : k + 1, :] == at, vals[k : k + 1, :] * SCALE, 0.0)
            if block == 0:
                total = total * keep_before
            elif block == 2:
                total = total * keep_after
            else:
                total = total + jnp.where(iota((step, V), 1) == at - V, diag, 0.0)
            hi, lo = cut2(total)
            hi_ref[block * V + j0 : block * V + j0 + step, :] = hi
            lo_ref[block * V + j0 : block * V + j0 + step, :] = lo


def kernel(
    counts_h, rate_h, ri_h, pi_h, leap_h, dr_h, fw_h, ft_h, rr_h, dn_h, tt_h, tv_h, ta_h, v_h, m_h, mc_h, mv_h,
    out_h, vnew,
    counts, rate, ri, pi, leap, dr, fw, ft, rrow, dn, tt, tv, ta, v, m, mc, mv,
    xs, sel, fire, am, ot, loc, rt, fb, rb, tb, vb, bh, bl, nh, nl, arr, cnew,
    slots, slots_in, pk1, rx1, nc, nv, nm, pk2, rx2, red, red_a, red_b,
    in_sem, out_sem, send_sem, recv_sem, relay_sem,
):
    me = lax.axis_index("dom")
    hbm = (counts_h, rate_h, ri_h, pi_h, leap_h, dr_h, fw_h, ft_h, rr_h, dn_h, tt_h, tv_h, ta_h, v_h, m_h, mc_h, mv_h)
    vmem = (counts, rate, ri, pi, leap, dr, fw, ft, rrow, dn, tt, tv, ta, v, m, mc, mv)
    loads = [pltpu.make_async_copy(h, d, in_sem.at[i]) for i, (h, d) in enumerate(zip(hbm, vmem))]
    for i in (7, 2, 3, 1, 0, 4, 5, 6, 9, 8, 10, 11, 12, 13, 14, 15, 16):
        loads[i].start()

    def chain(offset):
        return lax.rem(me + (offset + N), N)

    z_base = (me // ZG) * ZG
    z_at = lax.rem(me, ZG)
    xy_at = me // ZG

    def z_partner(j):
        return z_base + lax.rem(z_at + j, ZG)

    def xy_partner(j):
        x = lax.rem(xy_at // XY_SIDE + j // XY_SIDE, XY_SIDE)
        y = lax.rem(lax.rem(xy_at, XY_SIDE) + j % XY_SIDE, XY_SIDE)
        return (x * XY_SIDE + y) * ZG + z_at

    def z_chip(h):
        return z_base + lax.rem(z_at + 2 * h, ZG)

    barrier = pltpu.get_barrier_semaphore()
    other_core = 1 - 2 * lax.rem(me, 2)
    greet = [chain(o) for o in (3, -3, 2, -2, 1, -1)] + [xy_partner(j) for j in NEAR_XY]
    greet += [z_chip(h) for h in NEAR_Z] + [z_chip(h) + other_core for h in NEAR_Z] + [me + other_core]
    for other in greet:
        pl.semaphore_signal(barrier, inc=1, device_id=(other,), device_id_type=MESH)

    loads[7].wait()

    for f in range(4):
        fb[:, f * T : (f + 1) * T] = low_hot(ft[f : f + 1, :])

    for i in (1, 2, 3):
        loads[i].wait()
    lane = iota((1, 256), 1)
    wanted = jnp.where(lane < 3 * S, lax.rem(lane, S), jnp.where(lane == 3 * S, S, -1)).astype(F32)
    first = column(ri[0:1, :].astype(F32))
    second = column(ri[1:2, :].astype(F32))
    rates = column(rate[...])
    sel[:, 0:256] = hot(first == wanted)
    sel[:, 256:] = hot(second == wanted)
    cap_first = jnp.where(first == S, BIG, 0.0)
    cap_second = jnp.where(second == S, BIG, 0.0)
    level = iota((S, R), 0)

    def has(row):
        return jnp.where(row == level, 1.0, 0.0)

    stoich = (has(pi[0:1, :]) + has(pi[1:2, :]) - has(ri[0:1, :]) - has(ri[1:2, :])).astype(BF16)
    def build_targets(c, carry):
        at = iota((64, T), 0) + c * 64
        start = pl.multiple_of(c * 64, 64)
        for f in range(4):
            ot[pl.ds(start, 64), f * T : (f + 1) * T] = hot(ft[f : f + 1, :] == at)
        return carry

    lax.fori_loop(0, T // 64, build_targets, 0)
    loads[0].wait()
    for i, part in enumerate(cut3(counts[...])):
        xs[i * S : (i + 1) * S, :] = part
    xs[3 * S :, :] = jnp.ones((S, T), BF16)
    loads[4].wait()
    step = 64
    for c in range(0, R, step):
        x1 = nn(sel[c : c + step, 0:256], xs[...])
        x2 = nn(sel[c : c + step, 256:], xs[...])
        prop = rates[c : c + step, :] * x1 * x2
        limit = jnp.minimum(
            jnp.maximum(x1, cap_first[c : c + step, :]), jnp.maximum(x2, cap_second[c : c + step, :])
        )
        raw = prop + jnp.sqrt(prop) * leap[c : c + step, :].astype(F32)
        hi, lo = cut2(jnp.minimum(jnp.maximum(raw, 0.0), limit))
        fire[c : c + step, :] = hi
        fire[R + c : R + c + step, :] = lo
    delta = nn(stoich, fire[0:R, :]) + nn(stoich, fire[R:, :])
    cnew[...] = jnp.maximum(counts[...] + delta, 0.0)

    for i in (5, 6, 9):
        loads[i].wait()
    wall = T + 2 * B
    here = cnew[0:1, :]
    prob = dr[0:1, 0:1] * fw[...]
    mean = here * prob
    noise = jnp.concatenate([dn[f, 0:1, :].astype(F32) for f in range(4)], axis=0)
    raw = jnp.maximum(mean + jnp.sqrt(mean * (1.0 - prob)) * noise, 0.0)
    raw = jnp.where(ft[...] == wall, 0.0, raw)
    total = add_rows(raw)
    factor = jnp.minimum(1.0, here / jnp.maximum(total, 1.0))
    stays = here - total * factor
    leaves = [by_block(raw[f : f + 1, :] * factor, ft[f : f + 1, :]) for f in range(4)]
    out = groups(nt(jnp.concatenate(leaves, axis=1), fb[...]))
    own = out + jnp.concatenate([stays[:, a * 128 : (a + 1) * 128] for a in range(4)] * 2, axis=0)
    for side in range(2):
        for a in range(2):
            row = T // 128 + 2 * side + a
            pk1[side, :, a * 128 : (a + 1) * 128] = out[row : row + 1, :]
    loads[13].wait()
    for side in range(2):
        pk1[side, :, B:] = v[...]

    for i in (14, 15, 16):
        loads[i].wait()
    pl.semaphore_wait(barrier, len(greet))
    sends = []

    def send(src, dst, sem, other):
        copy = pltpu.make_async_remote_copy(
            src_ref=src, dst_ref=dst, send_sem=send_sem.at[sem], recv_sem=recv_sem.at[sem],
            device_id=(other,), device_id_type=MESH,
        )
        copy.start()
        sends.append(copy)
        return copy

    before, after = chain(-1), chain(1)
    def relay(others, level):
        for other in others:
            pl.semaphore_signal(relay_sem.at[level], inc=1, device_id=(other,), device_id_type=MESH)

    small = [send(pk1.at[1], rx1.at[0], 0, after), send(pk1.at[0], rx1.at[1], 1, before)]
    relay([z_chip(HOPS), z_chip(ZG // 2 - HOPS)], 0)
    relay([xy_partner(j) for j in XY_MIDDLE], 1)
    params = [send(mc, nc, 2, before), send(mv, nv, 3, before), send(m, nm, 4, before)]

    for i in (8, 10, 11, 12):
        loads[i].wait()
    recv = jnp.concatenate([rrow[0:1, :], rrow[1:2, :]], axis=1)
    rb[...] = low_hot(recv)
    tb[...] = low_hot(tt[...])
    for c in range(3):
        vb[:, c * T : (c + 1) * T] = low_hot(tv[c : c + 1, :])

    def flag(cond):
        return jnp.where(cond, 1.0, 0.0).astype(F32)

    has_before, has_after = flag(me > 0), flag(me < N - 1)
    build_matrix(mc, mv, m, has_before, has_after, bh, bl)

    lax.fori_loop(T // 64, (T + 2 * B) // 64, build_targets, 0)

    def apply(x, hi_ref, lo_ref, start=0):
        parts = rows3(x)
        size = x.shape[1]
        out = nn(parts, hi_ref[start : start + size, :]) + nn(parts, lo_ref[start : start + size, :])
        return add_rows(out)

    for copy in small:
        copy.wait_recv()
    arrived = jnp.concatenate([rx1[0, :, 0:B], rx1[1, :, 0:B]], axis=1)
    c0 = own + groups(nt(by_block(arrived, recv), rb[...]))
    parts = jnp.concatenate(split3(c0) + (jnp.zeros((8, 128), F32),), axis=0).astype(BF16)
    picked = groups(nn(parts, tb[...]))
    calcium = add_rows(jnp.where((tt[...] >> 7) == iota((8, T), 0), picked, 0.0))
    share = 4.0 * ta[...] * calcium / (calcium + 2.0) / 3.0
    corners = jnp.concatenate([by_block(share, tv[c : c + 1, :]) for c in range(3)], axis=1)
    given = groups(nt(corners, vb[...]))
    around = jnp.concatenate([rx1[0, :, B:], v[...], rx1[1, :, B:]], axis=1)
    start = m[...] * v[...] - apply(around, bh, bl) * (1.0 / SCALE)
    for a in range(2):
        half = slice(a * 128, (a + 1) * 128)
        pk2[:, half] = start[:, half] + given[2 + a : 3 + a, :]
        pk2[:, V + a * 128 : V + (a + 1) * 128] = given[a : a + 1, :]
        pk2[:, 2 * V + a * 128 : 2 * V + (a + 1) * 128] = given[4 + a : 5 + a, :]

    parts2 = [send(pk2, rx2.at[i], 7 + i, chain(-o)) for i, o in enumerate((-2, -1, 1, 2, 3))]

    pl.semaphore_wait(relay_sem.at[0], 2)
    relay([z_chip(2 * HOPS), z_chip(ZG // 2 - 2 * HOPS)], 2)
    for copy in params:
        copy.wait_recv()
    build_matrix(nc, nv, nm, 1.0, flag(me < N - 2), nh, nl)
    for copy in parts2:
        copy.wait_recv()
    own_e, own_b, own_a = pk2[:, 0:V], pk2[:, V : 2 * V], pk2[:, 2 * V :]
    r_own = own_e + rx2[1, :, 2 * V :] + rx2[2, :, V : 2 * V]
    r_before = rx2[1, :, 0:V] + own_b + rx2[0, :, 2 * V :]
    r_after = rx2[2, :, 0:V] + own_a + rx2[3, :, V : 2 * V]
    r_after2 = rx2[3, :, 0:V] + rx2[2, :, 2 * V :] + rx2[4, :, V : 2 * V]
    u_own = apply(jnp.concatenate([r_before, r_own, r_after], axis=1), bh, bl)
    u_after = apply(jnp.concatenate([r_own, r_after, r_after2], axis=1), nh, nl)
    t_own = apply(jnp.concatenate([u_own, 2.0 * u_after], axis=1), bh, bl, V)

    def fold(x):
        return x[:, 0:128] + x[:, 128:256]

    products = (fold(r_own * r_own), fold(r_own * u_own), fold(u_own * u_own), fold(u_own * t_own))
    at = iota((8, 128), 0)
    stack = jnp.zeros((8, 128), F32)
    for i, p in enumerate(products):
        stack = jnp.where(at == i, p, stack)
    sums = jnp.sum(stack, axis=1, keepdims=True)
    red[0] = add_rows(jnp.where(at == iota((8, 128), 1), sums, 0.0))

    def reduce(stage, partner, order, buffer, sem):
        for j in order:
            pltpu.make_async_remote_copy(
                src_ref=red.at[stage], dst_ref=buffer.at[j - 1], send_sem=send_sem.at[sem],
                recv_sem=recv_sem.at[sem], device_id=(partner(j),), device_id_type=MESH,
            ).start()

    pl.semaphore_wait(relay_sem.at[2], 2)
    reduce(0, z_partner, Z_ORDER, red_a, 12)


    hop = column(dr[...])
    step = 16
    for c in range(0, S, step):
        here = cnew[c : c + step, :]
        raws = []
        for f in range(4):
            prob = hop[c : c + step, :] * fw[f : f + 1, :]
            mean = here * prob
            spread = jnp.sqrt(mean * (1.0 - prob))
            raw = jnp.maximum(mean + spread * dn[f, c : c + step, :].astype(F32), 0.0)
            raws.append(jnp.where(ft[f : f + 1, :] == wall, 0.0, raw))
        total = raws[0] + raws[1] + raws[2] + raws[3]
        factor = jnp.minimum(1.0, here / jnp.maximum(total, 1.0))
        for f in range(4):
            hi, lo = cut2(raws[f] * factor)
            am[c : c + step, f * T : (f + 1) * T] = hi
            am[S + c : S + c + step, f * T : (f + 1) * T] = lo
        loc[c : c + step, :] = here - total * factor
    for side in range(2):
        out = nt(ot[T + side * B : T + (side + 1) * B, :], am[...]).T
        slots[side] = out[:S, :] + out[S:, :]
    bulk = [send(slots.at[1], slots_in.at[0], 5, after), send(slots.at[0], slots_in.at[1], 6, before)]

    pltpu.make_async_copy(red_a, red_a, recv_sem.at[12]).wait()
    red[1] = red[0] + jnp.sum(red_a[...], axis=0)
    pl.semaphore_wait(relay_sem.at[1], 2)
    reduce(1, xy_partner, XY_ORDER, red_b, 13)

    for w in range(0, T, 256):
        out = nt(ot[w : w + 256, :], am[...]).T
        loc[:, w : w + 256] = loc[:, w : w + 256] + out[:S, :] + out[S:, :]
    for c in range(0, T, 64):
        at = iota((64, B), 0) + c
        rt[c : c + 64, 0:B] = hot(rrow[0:1, :] == at)
        rt[c : c + 64, B:] = hot(rrow[1:2, :] == at)

    for copy in bulk:
        copy.wait_recv()
    for side in range(2):
        hi, lo = cut2(slots_in[side])
        arr[0:S, side * B : (side + 1) * B] = hi
        arr[S:, side * B : (side + 1) * B] = lo
    for w in range(0, T, 256):
        out = nt(rt[w : w + 256, :], arr[...]).T
        cnew[:, w : w + 256] = loc[:, w : w + 256] + out[:S, :] + out[S:, :]

    out_copy = pltpu.make_async_copy(cnew, out_h, out_sem)
    out_copy.start()

    pltpu.make_async_copy(red_b, red_b, recv_sem.at[13]).wait()
    final = red[1] + jnp.sum(red_b[...], axis=0)
    rr, ru, uu, ut = (final[:, i : i + 1] for i in range(4))
    alpha0 = rr / ru
    norm1 = alpha0 * alpha0 * uu - rr
    keep = 1.0 + norm1 / rr
    curve = keep * keep * ru - 2.0 * keep * alpha0 * uu + alpha0 * alpha0 * ut
    alpha1 = norm1 / curve
    direction = keep * r_own - alpha0 * u_own
    vnew[...] = v[...] + (alpha0 * SCALE) * r_own + (alpha1 * SCALE) * direction
    for copy in sends:
        copy.wait_send()
    pltpu.make_async_copy(red_a, red_a, send_sem.at[12]).wait()
    pltpu.make_async_copy(red_b, red_b, send_sem.at[13]).wait()
    out_copy.wait()


def finish(counts_in, v_in, counts_out, v_out, hold, hold_v, in_sem, out_sem):
    rows = S // PIECES
    parts = [slice(i * rows, (i + 1) * rows) for i in range(PIECES)]
    loads = [pltpu.make_async_copy(v_in, hold_v, in_sem.at[PIECES])]
    stores = [pltpu.make_async_copy(hold_v, v_out, out_sem.at[PIECES])]
    for i, part in enumerate(parts):
        loads.append(pltpu.make_async_copy(counts_in.at[part, :], hold.at[part, :], in_sem.at[i]))
        stores.append(pltpu.make_async_copy(hold.at[part, :], counts_out.at[part, :], out_sem.at[i]))
    for copy in loads:
        copy.start()
    for load, store in zip(loads, stores):
        load.wait()
        store.start()
    for copy in stores:
        copy.wait()


def per_device(*args):
    shaped = [a.reshape(1, -1) if a.ndim == 1 else a for a in args]
    any_spec = pl.BlockSpec(memory_space=pl.ANY)
    scratch = [pltpu.VMEM(a.shape, a.dtype) for a in shaped]
    scratch += [
        pltpu.VMEM((256, T), BF16),
        pltpu.VMEM((R, 512), BF16),
        pltpu.VMEM((2 * R, T), BF16),
        pltpu.VMEM((2 * S, 4 * T), BF16),
        pltpu.VMEM((T + 2 * B, 4 * T), BF16),
        pltpu.VMEM((S, T), F32),
        pltpu.VMEM((T, 2 * B), BF16),
        pltpu.VMEM((128, 4 * T), BF16),
        pltpu.VMEM((128, 2 * B), BF16),
        pltpu.VMEM((128, T), BF16),
        pltpu.VMEM((128, 3 * T), BF16),
        pltpu.VMEM((3 * V, V), BF16),
        pltpu.VMEM((3 * V, V), BF16),
        pltpu.VMEM((3 * V, V), BF16),
        pltpu.VMEM((3 * V, V), BF16),
        pltpu.VMEM((2 * S, 2 * B), BF16),
        pltpu.VMEM((S, T), F32),
        pltpu.VMEM((2, S, B), F32),
        pltpu.VMEM((2, S, B), F32),
        pltpu.VMEM((2, 1, B + V), F32),
        pltpu.VMEM((2, 1, B + V), F32),
        pltpu.VMEM((8, V), I32),
        pltpu.VMEM((8, V), F32),
        pltpu.VMEM((1, V), F32),
        pltpu.VMEM((1, 3 * V), F32),
        pltpu.VMEM((5, 1, 3 * V), F32),
        pltpu.VMEM((2, 1, 128), F32),
        pltpu.VMEM((ZG - 1, 1, 128), F32),
        pltpu.VMEM((XY - 1, 1, 128), F32),
        pltpu.SemaphoreType.DMA((17,)),
        pltpu.SemaphoreType.DMA,
        pltpu.SemaphoreType.DMA((14,)),
        pltpu.SemaphoreType.DMA((14,)),
        pltpu.SemaphoreType.REGULAR((3,)),
    ]
    counts_new, voltage = pl.pallas_call(
        kernel,
        name="step",
        out_shape=(jax.ShapeDtypeStruct((S, T), F32), jax.ShapeDtypeStruct((1, V), F32)),
        in_specs=[any_spec] * len(shaped),
        out_specs=(any_spec, pl.BlockSpec(memory_space=pltpu.VMEM)),
        scratch_shapes=scratch,
        compiler_params=pltpu.CompilerParams(
            collective_id=1, has_side_effects=True, vmem_limit_bytes=60 * 1024 * 1024
        ),
    )(*shaped)
    counts_new, voltage = pl.pallas_call(
        finish,
        name="finish",
        out_shape=(jax.ShapeDtypeStruct((S, T), F32), jax.ShapeDtypeStruct((1, V), F32)),
        in_specs=[any_spec, any_spec],
        out_specs=(any_spec, any_spec),
        scratch_shapes=[
            pltpu.VMEM((S, T), F32),
            pltpu.VMEM((1, V), F32),
            pltpu.SemaphoreType.DMA((PIECES + 1,)),
            pltpu.SemaphoreType.DMA((PIECES + 1,)),
        ],
        compiler_params=pltpu.CompilerParams(vmem_limit_bytes=60 * 1024 * 1024),
    )(counts_new, voltage)
    return counts_new, voltage.reshape(-1)


def solution(mesh):
    placed = (
        P(None, "dom"), P(), P(), P(), P(None, "dom"), P(), P(None, "dom"), P(None, "dom"), P(None, "dom"),
        P(None, None, "dom"), P("dom"), P(None, "dom"), P("dom"), P("dom"), P("dom"), P(None, "dom"),
        P(None, "dom"),
    )
    return jax.shard_map(
        per_device, mesh=mesh, in_specs=placed, out_specs=(P(None, "dom"), P("dom")), check_vma=False
    )
```

```python
import jax
import jax.numpy as jnp
from jax import lax
from jax.experimental import pallas as pl
from jax.experimental.pallas import tpu as pltpu
from jax.sharding import PartitionSpec as P

F32 = jnp.float32
BF16 = jnp.bfloat16
I32 = jnp.int32
MESH = pl.DeviceIdType.MESH

N = 512
S = 64
R = 256
T = 512
B = 256
V = 256
BIG = 1e30
SCALE = 1.0 / 32.0
ZG = 32
XY = 16


HOPS = 2
XY_SIDE = 4
PIECES = 2
NEAR_Z = [h for d in range(HOPS, 0, -1) for h in (d, ZG // 2 - d)]


def away(j, sizes):
    total = 0
    for size in reversed(sizes):
        total += min(j % size, size - j % size)
        j //= size
    return total


Z_ORDER = sorted(range(1, ZG), key=lambda j: -away(j // 2, (16,)))
XY_ORDER = sorted(range(1, XY), key=lambda j: -away(j, (XY_SIDE, XY_SIDE)))
NEAR_XY = [j for j in XY_ORDER if away(j, (XY_SIDE, XY_SIDE)) <= HOPS]
XY_MIDDLE = (2 * XY_SIDE, 2)


def nn(a, b):
    return lax.dot_general(a, b, (((1,), (0,)), ((), ())), preferred_element_type=F32)


def nt(a, b):
    return lax.dot_general(a, b, (((1,), (1,)), ((), ())), preferred_element_type=F32)


def iota(shape, dim):
    return lax.broadcasted_iota(I32, shape, dim)


def cut2(x):
    hi = x.astype(BF16)
    return hi, (x - hi.astype(F32)).astype(BF16)


def cut3(x):
    hi = x.astype(BF16)
    rest = x - hi.astype(F32)
    mid = rest.astype(BF16)
    return hi, mid, (rest - mid.astype(F32)).astype(BF16)


def rows3(x):
    hi = x.astype(BF16).astype(F32)
    rest = x - hi
    mid = rest.astype(BF16).astype(F32)
    low = rest - mid
    at = iota((16, x.shape[1]), 0)
    return jnp.where(at == 0, hi, jnp.where(at == 1, mid, jnp.where(at == 2, low, 0.0))).astype(BF16)


def add_rows(x):
    return jnp.sum(x, axis=0, keepdims=True)


def column(row):
    size = min(row.shape[1], 128)
    same = iota((size, size), 0) == iota((size, size), 1)
    blocks = [
        jnp.sum(jnp.where(same, row[:, at : at + size], 0.0), axis=1, keepdims=True)
        for at in range(0, row.shape[1], size)
    ]
    return blocks[0] if len(blocks) == 1 else jnp.concatenate(blocks, axis=0)


def split3(x):
    hi = x.astype(BF16).astype(F32)
    rest = x - hi
    mid = rest.astype(BF16).astype(F32)
    return hi, mid, rest - mid


def by_block(x, index):
    at = (index >> 7) == iota((8, x.shape[1]), 0)
    parts = [jnp.where(at, part, 0.0) for part in split3(x)]
    return jnp.concatenate(parts + [jnp.zeros((8, x.shape[1]), F32)], axis=0).astype(BF16)


def low_hot(index):
    return hot((index & 127) == iota((128, index.shape[1]), 0))


def groups(x):
    return x[0:8, :] + x[8:16, :] + x[16:24, :]


def hot(cond):
    return jnp.where(cond, 1.0, 0.0).astype(BF16)


def build_matrix(cols, vals, mass, keep_before, keep_after, hi_ref, lo_ref):
    diag = (mass[...] + jnp.sum(jnp.abs(vals[...]), axis=0, keepdims=True)) * SCALE
    step = 64
    for block, slots in ((0, (6, 7)), (1, (0, 1, 4, 5)), (2, (2, 3))):
        for j0 in range(0, V, step):
            at = iota((step, V), 0) + (block * V + j0)
            total = jnp.zeros((step, V), F32)
            for k in slots:
                total = total + jnp.where(cols[k : k + 1, :] == at, vals[k : k + 1, :] * SCALE, 0.0)
            if block == 0:
                total = total * keep_before
            elif block == 2:
                total = total * keep_after
            else:
                total = total + jnp.where(iota((step, V), 1) == at - V, diag, 0.0)
            hi, lo = cut2(total)
            hi_ref[block * V + j0 : block * V + j0 + step, :] = hi
            lo_ref[block * V + j0 : block * V + j0 + step, :] = lo


def kernel(
    counts_h, rate_h, ri_h, pi_h, leap_h, dr_h, fw_h, ft_h, rr_h, dn_h, tt_h, tv_h, ta_h, v_h, m_h, mc_h, mv_h,
    out_h, vnew,
    counts, rate, ri, pi, leap, dr, fw, ft, rrow, dn, tt, tv, ta, v, m, mc, mv,
    xs, sel, fire, am, ot, loc, rt, fb, rb, tb, vb, bh, bl, nh, nl, arr, cnew,
    slots, slots_in, pk1, rx1, nc, nv, nm, pk2, rx2, red, red_a, red_b,
    in_sem, out_sem, send_sem, recv_sem, relay_sem,
):
    me = lax.axis_index("dom")
    hbm = (counts_h, rate_h, ri_h, pi_h, leap_h, dr_h, fw_h, ft_h, rr_h, dn_h, tt_h, tv_h, ta_h, v_h, m_h, mc_h, mv_h)
    vmem = (counts, rate, ri, pi, leap, dr, fw, ft, rrow, dn, tt, tv, ta, v, m, mc, mv)
    loads = [pltpu.make_async_copy(h, d, in_sem.at[i]) for i, (h, d) in enumerate(zip(hbm, vmem))]
    for i in (7, 2, 3, 1, 0, 4, 5, 6, 9, 8, 10, 11, 12, 13, 14, 15, 16):
        loads[i].start()

    def chain(offset):
        return lax.rem(me + (offset + N), N)

    z_base = (me // ZG) * ZG
    z_at = lax.rem(me, ZG)
    xy_at = me // ZG

    def z_partner(j):
        return z_base + lax.rem(z_at + j, ZG)

    def xy_partner(j):
        x = lax.rem(xy_at // XY_SIDE + j // XY_SIDE, XY_SIDE)
        y = lax.rem(lax.rem(xy_at, XY_SIDE) + j % XY_SIDE, XY_SIDE)
        return (x * XY_SIDE + y) * ZG + z_at

    def z_chip(h):
        return z_base + lax.rem(z_at + 2 * h, ZG)

    barrier = pltpu.get_barrier_semaphore()
    other_core = 1 - 2 * lax.rem(me, 2)
    greet = [chain(o) for o in (3, -3, 2, -2, 1, -1)] + [xy_partner(j) for j in NEAR_XY]
    greet += [z_chip(h) for h in NEAR_Z] + [z_chip(h) + other_core for h in NEAR_Z] + [me + other_core]
    for other in greet:
        pl.semaphore_signal(barrier, inc=1, device_id=(other,), device_id_type=MESH)

    loads[7].wait()

    for f in range(4):
        fb[:, f * T : (f + 1) * T] = low_hot(ft[f : f + 1, :])

    for i in (1, 2, 3):
        loads[i].wait()
    lane = iota((1, 256), 1)
    wanted = jnp.where(lane < 3 * S, lax.rem(lane, S), jnp.where(lane == 3 * S, S, -1)).astype(F32)
    first = column(ri[0:1, :].astype(F32))
    second = column(ri[1:2, :].astype(F32))
    rates = column(rate[...])
    sel[:, 0:256] = hot(first == wanted)
    sel[:, 256:] = hot(second == wanted)
    cap_first = jnp.where(first == S, BIG, 0.0)
    cap_second = jnp.where(second == S, BIG, 0.0)
    level = iota((S, R), 0)

    def has(row):
        return jnp.where(row == level, 1.0, 0.0)

    stoich = (has(pi[0:1, :]) + has(pi[1:2, :]) - has(ri[0:1, :]) - has(ri[1:2, :])).astype(BF16)
    def build_targets(c, carry):
        at = iota((64, T), 0) + c * 64
        start = pl.multiple_of(c * 64, 64)
        for f in range(4):
            ot[pl.ds(start, 64), f * T : (f + 1) * T] = hot(ft[f : f + 1, :] == at)
        return carry

    lax.fori_loop(0, T // 64, build_targets, 0)
    loads[0].wait()
    for i, part in enumerate(cut3(counts[...])):
        xs[i * S : (i + 1) * S, :] = part
    xs[3 * S :, :] = jnp.ones((S, T), BF16)
    loads[4].wait()
    step = 64
    for c in range(0, R, step):
        x1 = nn(sel[c : c + step, 0:256], xs[...])
        x2 = nn(sel[c : c + step, 256:], xs[...])
        prop = rates[c : c + step, :] * x1 * x2
        limit = jnp.minimum(
            jnp.maximum(x1, cap_first[c : c + step, :]), jnp.maximum(x2, cap_second[c : c + step, :])
        )
        raw = prop + jnp.sqrt(prop) * leap[c : c + step, :].astype(F32)
        hi, lo = cut2(jnp.minimum(jnp.maximum(raw, 0.0), limit))
        fire[c : c + step, :] = hi
        fire[R + c : R + c + step, :] = lo
    delta = nn(stoich, fire[0:R, :]) + nn(stoich, fire[R:, :])
    cnew[...] = jnp.maximum(counts[...] + delta, 0.0)

    for i in (5, 6, 9):
        loads[i].wait()
    wall = T + 2 * B
    here = cnew[0:1, :]
    prob = dr[0:1, 0:1] * fw[...]
    mean = here * prob
    noise = jnp.concatenate([dn[f, 0:1, :].astype(F32) for f in range(4)], axis=0)
    raw = jnp.maximum(mean + jnp.sqrt(mean * (1.0 - prob)) * noise, 0.0)
    raw = jnp.where(ft[...] == wall, 0.0, raw)
    total = add_rows(raw)
    factor = jnp.minimum(1.0, here / jnp.maximum(total, 1.0))
    stays = here - total * factor
    leaves = [by_block(raw[f : f + 1, :] * factor, ft[f : f + 1, :]) for f in range(4)]
    out = groups(nt(jnp.concatenate(leaves, axis=1), fb[...]))
    own = out + jnp.concatenate([stays[:, a * 128 : (a + 1) * 128] for a in range(4)] * 2, axis=0)
    for side in range(2):
        for a in range(2):
            row = T // 128 + 2 * side + a
            pk1[side, :, a * 128 : (a + 1) * 128] = out[row : row + 1, :]
    loads[13].wait()
    for side in range(2):
        pk1[side, :, B:] = v[...]

    for i in (14, 15, 16):
        loads[i].wait()
    pl.semaphore_wait(barrier, len(greet))
    sends = []

    def send(src, dst, sem, other):
        copy = pltpu.make_async_remote_copy(
            src_ref=src, dst_ref=dst, send_sem=send_sem.at[sem], recv_sem=recv_sem.at[sem],
            device_id=(other,), device_id_type=MESH,
        )
        copy.start()
        sends.append(copy)
        return copy

    before, after = chain(-1), chain(1)
    def relay(others, level):
        for other in others:
            pl.semaphore_signal(relay_sem.at[level], inc=1, device_id=(other,), device_id_type=MESH)

    small = [send(pk1.at[1], rx1.at[0], 0, after), send(pk1.at[0], rx1.at[1], 1, before)]
    relay([z_chip(HOPS), z_chip(ZG // 2 - HOPS)], 0)
    relay([xy_partner(j) for j in XY_MIDDLE], 1)
    params = [send(mc, nc, 2, before), send(mv, nv, 3, before), send(m, nm, 4, before)]

    for i in (8, 10, 11, 12):
        loads[i].wait()
    recv = jnp.concatenate([rrow[0:1, :], rrow[1:2, :]], axis=1)
    rb[...] = low_hot(recv)
    tb[...] = low_hot(tt[...])
    for c in range(3):
        vb[:, c * T : (c + 1) * T] = low_hot(tv[c : c + 1, :])

    def flag(cond):
        return jnp.where(cond, 1.0, 0.0).astype(F32)

    has_before, has_after = flag(me > 0), flag(me < N - 1)
    build_matrix(mc, mv, m, has_before, has_after, bh, bl)

    lax.fori_loop(T // 64, (T + 2 * B) // 64, build_targets, 0)

    def apply(x, hi_ref, lo_ref, start=0):
        parts = rows3(x)
        size = x.shape[1]
        out = nn(parts, hi_ref[start : start + size, :]) + nn(parts, lo_ref[start : start + size, :])
        return add_rows(out)

    for copy in small:
        copy.wait_recv()
    arrived = jnp.concatenate([rx1[0, :, 0:B], rx1[1, :, 0:B]], axis=1)
    c0 = own + groups(nt(by_block(arrived, recv), rb[...]))
    parts = jnp.concatenate(split3(c0) + (jnp.zeros((8, 128), F32),), axis=0).astype(BF16)
    picked = groups(nn(parts, tb[...]))
    calcium = add_rows(jnp.where((tt[...] >> 7) == iota((8, T), 0), picked, 0.0))
    share = 4.0 * ta[...] * calcium / (calcium + 2.0) / 3.0
    corners = jnp.concatenate([by_block(share, tv[c : c + 1, :]) for c in range(3)], axis=1)
    given = groups(nt(corners, vb[...]))
    around = jnp.concatenate([rx1[0, :, B:], v[...], rx1[1, :, B:]], axis=1)
    start = m[...] * v[...] - apply(around, bh, bl) * (1.0 / SCALE)
    for a in range(2):
        half = slice(a * 128, (a + 1) * 128)
        pk2[:, half] = start[:, half] + given[2 + a : 3 + a, :]
        pk2[:, V + a * 128 : V + (a + 1) * 128] = given[a : a + 1, :]
        pk2[:, 2 * V + a * 128 : 2 * V + (a + 1) * 128] = given[4 + a : 5 + a, :]

    parts2 = [send(pk2, rx2.at[i], 7 + i, chain(-o)) for i, o in enumerate((-2, -1, 1, 2, 3))]

    pl.semaphore_wait(relay_sem.at[0], 2)
    relay([z_chip(2 * HOPS), z_chip(ZG // 2 - 2 * HOPS)], 2)
    for copy in params:
        copy.wait_recv()
    build_matrix(nc, nv, nm, 1.0, flag(me < N - 2), nh, nl)
    for copy in parts2:
        copy.wait_recv()
    own_e, own_b, own_a = pk2[:, 0:V], pk2[:, V : 2 * V], pk2[:, 2 * V :]
    r_own = own_e + rx2[1, :, 2 * V :] + rx2[2, :, V : 2 * V]
    r_before = rx2[1, :, 0:V] + own_b + rx2[0, :, 2 * V :]
    r_after = rx2[2, :, 0:V] + own_a + rx2[3, :, V : 2 * V]
    r_after2 = rx2[3, :, 0:V] + rx2[2, :, 2 * V :] + rx2[4, :, V : 2 * V]
    u_own = apply(jnp.concatenate([r_before, r_own, r_after], axis=1), bh, bl)
    u_after = apply(jnp.concatenate([r_own, r_after, r_after2], axis=1), nh, nl)
    t_own = apply(jnp.concatenate([u_own, 2.0 * u_after], axis=1), bh, bl, V)

    def fold(x):
        return x[:, 0:128] + x[:, 128:256]

    products = (fold(r_own * r_own), fold(r_own * u_own), fold(u_own * u_own), fold(u_own * t_own))
    at = iota((8, 128), 0)
    stack = jnp.zeros((8, 128), F32)
    for i, p in enumerate(products):
        stack = jnp.where(at == i, p, stack)
    sums = jnp.sum(stack, axis=1, keepdims=True)
    red[0] = add_rows(jnp.where(at == iota((8, 128), 1), sums, 0.0))

    def reduce(stage, partner, order, buffer, sem):
        for j in order:
            pltpu.make_async_remote_copy(
                src_ref=red.at[stage], dst_ref=buffer.at[j - 1], send_sem=send_sem.at[sem],
                recv_sem=recv_sem.at[sem], device_id=(partner(j),), device_id_type=MESH,
            ).start()

    pl.semaphore_wait(relay_sem.at[2], 2)
    reduce(0, z_partner, Z_ORDER, red_a, 12)


    hop = column(dr[...])
    step = 16
    for c in range(0, S, step):
        here = cnew[c : c + step, :]
        raws = []
        for f in range(4):
            prob = hop[c : c + step, :] * fw[f : f + 1, :]
            mean = here * prob
            spread = jnp.sqrt(mean * (1.0 - prob))
            raw = jnp.maximum(mean + spread * dn[f, c : c + step, :].astype(F32), 0.0)
            raws.append(jnp.where(ft[f : f + 1, :] == wall, 0.0, raw))
        total = raws[0] + raws[1] + raws[2] + raws[3]
        factor = jnp.minimum(1.0, here / jnp.maximum(total, 1.0))
        for f in range(4):
            hi, lo = cut2(raws[f] * factor)
            am[c : c + step, f * T : (f + 1) * T] = hi
            am[S + c : S + c + step, f * T : (f + 1) * T] = lo
        loc[c : c + step, :] = here - total * factor
    for side in range(2):
        out = nt(ot[T + side * B : T + (side + 1) * B, :], am[...]).T
        slots[side] = out[:S, :] + out[S:, :]

    pltpu.make_async_copy(red_a, red_a, recv_sem.at[12]).wait()
    red[1] = red[0] + jnp.sum(red_a[...], axis=0)
    pl.semaphore_wait(relay_sem.at[1], 2)
    reduce(1, xy_partner, XY_ORDER, red_b, 13)

    bulk = [send(slots.at[1], slots_in.at[0], 5, after), send(slots.at[0], slots_in.at[1], 6, before)]
    for w in range(0, T, 256):
        out = nt(ot[w : w + 256, :], am[...]).T
        loc[:, w : w + 256] = loc[:, w : w + 256] + out[:S, :] + out[S:, :]
    for c in range(0, T, 64):
        at = iota((64, B), 0) + c
        rt[c : c + 64, 0:B] = hot(rrow[0:1, :] == at)
        rt[c : c + 64, B:] = hot(rrow[1:2, :] == at)

    for copy in bulk:
        copy.wait_recv()
    for side in range(2):
        hi, lo = cut2(slots_in[side])
        arr[0:S, side * B : (side + 1) * B] = hi
        arr[S:, side * B : (side + 1) * B] = lo
    for w in range(0, T, 256):
        out = nt(rt[w : w + 256, :], arr[...]).T
        cnew[:, w : w + 256] = loc[:, w : w + 256] + out[:S, :] + out[S:, :]

    out_copy = pltpu.make_async_copy(cnew, out_h, out_sem)
    out_copy.start()

    pltpu.make_async_copy(red_b, red_b, recv_sem.at[13]).wait()
    final = red[1] + jnp.sum(red_b[...], axis=0)
    rr, ru, uu, ut = (final[:, i : i + 1] for i in range(4))
    alpha0 = rr / ru
    norm1 = alpha0 * alpha0 * uu - rr
    keep = 1.0 + norm1 / rr
    curve = keep * keep * ru - 2.0 * keep * alpha0 * uu + alpha0 * alpha0 * ut
    alpha1 = norm1 / curve
    direction = keep * r_own - alpha0 * u_own
    vnew[...] = v[...] + (alpha0 * SCALE) * r_own + (alpha1 * SCALE) * direction
    for copy in sends:
        copy.wait_send()
    pltpu.make_async_copy(red_a, red_a, send_sem.at[12]).wait()
    pltpu.make_async_copy(red_b, red_b, send_sem.at[13]).wait()
    out_copy.wait()


def finish(counts_in, v_in, counts_out, v_out, hold, hold_v, in_sem, out_sem):
    rows = S // PIECES
    parts = [slice(i * rows, (i + 1) * rows) for i in range(PIECES)]
    loads = [pltpu.make_async_copy(v_in, hold_v, in_sem.at[PIECES])]
    stores = [pltpu.make_async_copy(hold_v, v_out, out_sem.at[PIECES])]
    for i, part in enumerate(parts):
        loads.append(pltpu.make_async_copy(counts_in.at[part, :], hold.at[part, :], in_sem.at[i]))
        stores.append(pltpu.make_async_copy(hold.at[part, :], counts_out.at[part, :], out_sem.at[i]))
    for copy in loads:
        copy.start()
    for load, store in zip(loads, stores):
        load.wait()
        store.start()
    for copy in stores:
        copy.wait()


def per_device(*args):
    shaped = [a.reshape(1, -1) if a.ndim == 1 else a for a in args]
    any_spec = pl.BlockSpec(memory_space=pl.ANY)
    scratch = [pltpu.VMEM(a.shape, a.dtype) for a in shaped]
    scratch += [
        pltpu.VMEM((256, T), BF16),
        pltpu.VMEM((R, 512), BF16),
        pltpu.VMEM((2 * R, T), BF16),
        pltpu.VMEM((2 * S, 4 * T), BF16),
        pltpu.VMEM((T + 2 * B, 4 * T), BF16),
        pltpu.VMEM((S, T), F32),
        pltpu.VMEM((T, 2 * B), BF16),
        pltpu.VMEM((128, 4 * T), BF16),
        pltpu.VMEM((128, 2 * B), BF16),
        pltpu.VMEM((128, T), BF16),
        pltpu.VMEM((128, 3 * T), BF16),
        pltpu.VMEM((3 * V, V), BF16),
        pltpu.VMEM((3 * V, V), BF16),
        pltpu.VMEM((3 * V, V), BF16),
        pltpu.VMEM((3 * V, V), BF16),
        pltpu.VMEM((2 * S, 2 * B), BF16),
        pltpu.VMEM((S, T), F32),
        pltpu.VMEM((2, S, B), F32),
        pltpu.VMEM((2, S, B), F32),
        pltpu.VMEM((2, 1, B + V), F32),
        pltpu.VMEM((2, 1, B + V), F32),
        pltpu.VMEM((8, V), I32),
        pltpu.VMEM((8, V), F32),
        pltpu.VMEM((1, V), F32),
        pltpu.VMEM((1, 3 * V), F32),
        pltpu.VMEM((5, 1, 3 * V), F32),
        pltpu.VMEM((2, 1, 128), F32),
        pltpu.VMEM((ZG - 1, 1, 128), F32),
        pltpu.VMEM((XY - 1, 1, 128), F32),
        pltpu.SemaphoreType.DMA((17,)),
        pltpu.SemaphoreType.DMA,
        pltpu.SemaphoreType.DMA((14,)),
        pltpu.SemaphoreType.DMA((14,)),
        pltpu.SemaphoreType.REGULAR((3,)),
    ]
    counts_new, voltage = pl.pallas_call(
        kernel,
        name="step",
        out_shape=(jax.ShapeDtypeStruct((S, T), F32), jax.ShapeDtypeStruct((1, V), F32)),
        in_specs=[any_spec] * len(shaped),
        out_specs=(any_spec, pl.BlockSpec(memory_space=pltpu.VMEM)),
        scratch_shapes=scratch,
        compiler_params=pltpu.CompilerParams(
            collective_id=1, has_side_effects=True, vmem_limit_bytes=60 * 1024 * 1024
        ),
    )(*shaped)
    counts_new, voltage = pl.pallas_call(
        finish,
        name="finish",
        out_shape=(jax.ShapeDtypeStruct((S, T), F32), jax.ShapeDtypeStruct((1, V), F32)),
        in_specs=[any_spec, any_spec],
        out_specs=(any_spec, any_spec),
        scratch_shapes=[
            pltpu.VMEM((S, T), F32),
            pltpu.VMEM((1, V), F32),
            pltpu.SemaphoreType.DMA((PIECES + 1,)),
            pltpu.SemaphoreType.DMA((PIECES + 1,)),
        ],
        compiler_params=pltpu.CompilerParams(vmem_limit_bytes=60 * 1024 * 1024),
    )(counts_new, voltage)
    return counts_new, voltage.reshape(-1)


def solution(mesh):
    placed = (
        P(None, "dom"), P(), P(), P(), P(None, "dom"), P(), P(None, "dom"), P(None, "dom"), P(None, "dom"),
        P(None, None, "dom"), P("dom"), P(None, "dom"), P("dom"), P("dom"), P("dom"), P(None, "dom"),
        P(None, "dom"),
    )
    return jax.shard_map(
        per_device, mesh=mesh, in_specs=placed, out_specs=(P(None, "dom"), P("dom")), check_vma=False
    )
```

```python
import jax
import jax.numpy as jnp
from jax import lax
from jax.experimental import pallas as pl
from jax.experimental.pallas import tpu as pltpu
from jax.sharding import PartitionSpec as P

F32 = jnp.float32
BF16 = jnp.bfloat16
I32 = jnp.int32
MESH = pl.DeviceIdType.MESH

N = 512
S = 64
R = 256
T = 512
B = 256
V = 256
BIG = 1e30
SCALE = 1.0 / 32.0
ZG = 32
XY = 16


HOPS = 2
XY_SIDE = 4
PIECES = 1
NEAR_Z = [h for d in range(HOPS, 0, -1) for h in (d, ZG // 2 - d)]


def away(j, sizes):
    total = 0
    for size in reversed(sizes):
        total += min(j % size, size - j % size)
        j //= size
    return total


Z_ORDER = sorted(range(1, ZG), key=lambda j: -away(j // 2, (16,)))
XY_ORDER = sorted(range(1, XY), key=lambda j: -away(j, (XY_SIDE, XY_SIDE)))
NEAR_XY = [j for j in XY_ORDER if away(j, (XY_SIDE, XY_SIDE)) <= HOPS]
XY_MIDDLE = (2 * XY_SIDE, 2)


def nn(a, b):
    return lax.dot_general(a, b, (((1,), (0,)), ((), ())), preferred_element_type=F32)


def nt(a, b):
    return lax.dot_general(a, b, (((1,), (1,)), ((), ())), preferred_element_type=F32)


def iota(shape, dim):
    return lax.broadcasted_iota(I32, shape, dim)


def cut2(x):
    hi = x.astype(BF16)
    return hi, (x - hi.astype(F32)).astype(BF16)


def cut3(x):
    hi = x.astype(BF16)
    rest = x - hi.astype(F32)
    mid = rest.astype(BF16)
    return hi, mid, (rest - mid.astype(F32)).astype(BF16)


def rows3(x):
    hi = x.astype(BF16).astype(F32)
    rest = x - hi
    mid = rest.astype(BF16).astype(F32)
    low = rest - mid
    at = iota((16, x.shape[1]), 0)
    return jnp.where(at == 0, hi, jnp.where(at == 1, mid, jnp.where(at == 2, low, 0.0))).astype(BF16)


def add_rows(x):
    return jnp.sum(x, axis=0, keepdims=True)


def column(row):
    size = min(row.shape[1], 128)
    same = iota((size, size), 0) == iota((size, size), 1)
    blocks = [
        jnp.sum(jnp.where(same, row[:, at : at + size], 0.0), axis=1, keepdims=True)
        for at in range(0, row.shape[1], size)
    ]
    return blocks[0] if len(blocks) == 1 else jnp.concatenate(blocks, axis=0)


def split3(x):
    hi = x.astype(BF16).astype(F32)
    rest = x - hi
    mid = rest.astype(BF16).astype(F32)
    return hi, mid, rest - mid


def by_block(x, index):
    at = (index >> 7) == iota((8, x.shape[1]), 0)
    parts = [jnp.where(at, part, 0.0) for part in split3(x)]
    return jnp.concatenate(parts + [jnp.zeros((8, x.shape[1]), F32)], axis=0).astype(BF16)


def low_hot(index):
    return hot((index & 127) == iota((128, index.shape[1]), 0))


def groups(x):
    return x[0:8, :] + x[8:16, :] + x[16:24, :]


def hot(cond):
    return jnp.where(cond, 1.0, 0.0).astype(BF16)


def build_matrix(cols, vals, mass, keep_before, keep_after, hi_ref, lo_ref):
    diag = (mass[...] + jnp.sum(jnp.abs(vals[...]), axis=0, keepdims=True)) * SCALE
    step = 64
    for block, slots in ((0, (6, 7)), (1, (0, 1, 4, 5)), (2, (2, 3))):
        for j0 in range(0, V, step):
            at = iota((step, V), 0) + (block * V + j0)
            total = jnp.zeros((step, V), F32)
            for k in slots:
                total = total + jnp.where(cols[k : k + 1, :] == at, vals[k : k + 1, :] * SCALE, 0.0)
            if block == 0:
                total = total * keep_before
            elif block == 2:
                total = total * keep_after
            else:
                total = total + jnp.where(iota((step, V), 1) == at - V, diag, 0.0)
            hi, lo = cut2(total)
            hi_ref[block * V + j0 : block * V + j0 + step, :] = hi
            lo_ref[block * V + j0 : block * V + j0 + step, :] = lo


def kernel(
    counts_h, rate_h, ri_h, pi_h, leap_h, dr_h, fw_h, ft_h, rr_h, dn_h, tt_h, tv_h, ta_h, v_h, m_h, mc_h, mv_h,
    out_h, vnew,
    counts, rate, ri, pi, leap, dr, fw, ft, rrow, dn, tt, tv, ta, v, m, mc, mv,
    xs, sel, fire, am, ot, loc, rt, fb, rb, tb, vb, bh, bl, nh, nl, arr, cnew,
    slots, slots_in, pk1, rx1, nc, nv, nm, pk2, rx2, red, red_a, red_b,
    in_sem, out_sem, send_sem, recv_sem, relay_sem,
):
    me = lax.axis_index("dom")
    hbm = (counts_h, rate_h, ri_h, pi_h, leap_h, dr_h, fw_h, ft_h, rr_h, dn_h, tt_h, tv_h, ta_h, v_h, m_h, mc_h, mv_h)
    vmem = (counts, rate, ri, pi, leap, dr, fw, ft, rrow, dn, tt, tv, ta, v, m, mc, mv)
    loads = [pltpu.make_async_copy(h, d, in_sem.at[i]) for i, (h, d) in enumerate(zip(hbm, vmem))]
    for i in (7, 2, 3, 1, 0, 4, 5, 6, 9, 8, 10, 11, 12, 13, 14, 15, 16):
        loads[i].start()

    def chain(offset):
        return lax.rem(me + (offset + N), N)

    z_base = (me // ZG) * ZG
    z_at = lax.rem(me, ZG)
    xy_at = me // ZG

    def z_partner(j):
        return z_base + lax.rem(z_at + j, ZG)

    def xy_partner(j):
        x = lax.rem(xy_at // XY_SIDE + j // XY_SIDE, XY_SIDE)
        y = lax.rem(lax.rem(xy_at, XY_SIDE) + j % XY_SIDE, XY_SIDE)
        return (x * XY_SIDE + y) * ZG + z_at

    def z_chip(h):
        return z_base + lax.rem(z_at + 2 * h, ZG)

    barrier = pltpu.get_barrier_semaphore()
    other_core = 1 - 2 * lax.rem(me, 2)
    greet = [chain(o) for o in (3, -3, 2, -2, 1, -1)] + [xy_partner(j) for j in NEAR_XY]
    greet += [z_chip(h) for h in NEAR_Z] + [z_chip(h) + other_core for h in NEAR_Z] + [me + other_core]
    for other in greet:
        pl.semaphore_signal(barrier, inc=1, device_id=(other,), device_id_type=MESH)

    loads[7].wait()

    for f in range(4):
        fb[:, f * T : (f + 1) * T] = low_hot(ft[f : f + 1, :])

    for i in (1, 2, 3):
        loads[i].wait()
    lane = iota((1, 256), 1)
    wanted = jnp.where(lane < 3 * S, lax.rem(lane, S), jnp.where(lane == 3 * S, S, -1)).astype(F32)
    first = column(ri[0:1, :].astype(F32))
    second = column(ri[1:2, :].astype(F32))
    rates = column(rate[...])
    sel[:, 0:256] = hot(first == wanted)
    sel[:, 256:] = hot(second == wanted)
    cap_first = jnp.where(first == S, BIG, 0.0)
    cap_second = jnp.where(second == S, BIG, 0.0)
    level = iota((S, R), 0)

    def has(row):
        return jnp.where(row == level, 1.0, 0.0)

    stoich = (has(pi[0:1, :]) + has(pi[1:2, :]) - has(ri[0:1, :]) - has(ri[1:2, :])).astype(BF16)
    loads[0].wait()
    for i, part in enumerate(cut3(counts[...])):
        xs[i * S : (i + 1) * S, :] = part
    xs[3 * S :, :] = jnp.ones((S, T), BF16)
    loads[4].wait()
    step = 64
    for c in range(0, R, step):
        x1 = nn(sel[c : c + step, 0:256], xs[...])
        x2 = nn(sel[c : c + step, 256:], xs[...])
        prop = rates[c : c + step, :] * x1 * x2
        limit = jnp.minimum(
            jnp.maximum(x1, cap_first[c : c + step, :]), jnp.maximum(x2, cap_second[c : c + step, :])
        )
        raw = prop + jnp.sqrt(prop) * leap[c : c + step, :].astype(F32)
        hi, lo = cut2(jnp.minimum(jnp.maximum(raw, 0.0), limit))
        fire[c : c + step, :] = hi
        fire[R + c : R + c + step, :] = lo
    delta = nn(stoich, fire[0:R, :]) + nn(stoich, fire[R:, :])
    cnew[...] = jnp.maximum(counts[...] + delta, 0.0)

    for i in (5, 6, 9):
        loads[i].wait()
    wall = T + 2 * B
    here = cnew[0:1, :]
    prob = dr[0:1, 0:1] * fw[...]
    mean = here * prob
    noise = jnp.concatenate([dn[f, 0:1, :].astype(F32) for f in range(4)], axis=0)
    raw = jnp.maximum(mean + jnp.sqrt(mean * (1.0 - prob)) * noise, 0.0)
    raw = jnp.where(ft[...] == wall, 0.0, raw)
    total = add_rows(raw)
    factor = jnp.minimum(1.0, here / jnp.maximum(total, 1.0))
    stays = here - total * factor
    leaves = [by_block(raw[f : f + 1, :] * factor, ft[f : f + 1, :]) for f in range(4)]
    out = groups(nt(jnp.concatenate(leaves, axis=1), fb[...]))
    own = out + jnp.concatenate([stays[:, a * 128 : (a + 1) * 128] for a in range(4)] * 2, axis=0)
    for side in range(2):
        for a in range(2):
            row = T // 128 + 2 * side + a
            pk1[side, :, a * 128 : (a + 1) * 128] = out[row : row + 1, :]
    loads[13].wait()
    for side in range(2):
        pk1[side, :, B:] = v[...]

    for i in (14, 15, 16):
        loads[i].wait()
    pl.semaphore_wait(barrier, len(greet))
    sends = []

    def send(src, dst, sem, other):
        copy = pltpu.make_async_remote_copy(
            src_ref=src, dst_ref=dst, send_sem=send_sem.at[sem], recv_sem=recv_sem.at[sem],
            device_id=(other,), device_id_type=MESH,
        )
        copy.start()
        sends.append(copy)
        return copy

    before, after = chain(-1), chain(1)
    def relay(others, level):
        for other in others:
            pl.semaphore_signal(relay_sem.at[level], inc=1, device_id=(other,), device_id_type=MESH)

    small = [send(pk1.at[1], rx1.at[0], 0, after), send(pk1.at[0], rx1.at[1], 1, before)]
    relay([z_chip(HOPS), z_chip(ZG // 2 - HOPS)], 0)
    relay([xy_partner(j) for j in XY_MIDDLE], 1)
    params = [send(mc, nc, 2, before), send(mv, nv, 3, before), send(m, nm, 4, before)]

    for i in (8, 10, 11, 12):
        loads[i].wait()
    recv = jnp.concatenate([rrow[0:1, :], rrow[1:2, :]], axis=1)
    rb[...] = low_hot(recv)
    tb[...] = low_hot(tt[...])
    for c in range(3):
        vb[:, c * T : (c + 1) * T] = low_hot(tv[c : c + 1, :])

    def flag(cond):
        return jnp.where(cond, 1.0, 0.0).astype(F32)

    has_before, has_after = flag(me > 0), flag(me < N - 1)
    build_matrix(mc, mv, m, has_before, has_after, bh, bl)

    def build_targets(c, carry):
        at = iota((64, T), 0) + c * 64
        start = pl.multiple_of(c * 64, 64)
        for f in range(4):
            ot[pl.ds(start, 64), f * T : (f + 1) * T] = hot(ft[f : f + 1, :] == at)
        return carry

    lax.fori_loop(0, (T + 2 * B) // 64, build_targets, 0)

    def apply(x, hi_ref, lo_ref, start=0):
        parts = rows3(x)
        size = x.shape[1]
        out = nn(parts, hi_ref[start : start + size, :]) + nn(parts, lo_ref[start : start + size, :])
        return add_rows(out)

    for copy in small:
        copy.wait_recv()
    arrived = jnp.concatenate([rx1[0, :, 0:B], rx1[1, :, 0:B]], axis=1)
    c0 = own + groups(nt(by_block(arrived, recv), rb[...]))
    parts = jnp.concatenate(split3(c0) + (jnp.zeros((8, 128), F32),), axis=0).astype(BF16)
    picked = groups(nn(parts, tb[...]))
    calcium = add_rows(jnp.where((tt[...] >> 7) == iota((8, T), 0), picked, 0.0))
    share = 4.0 * ta[...] * calcium / (calcium + 2.0) / 3.0
    corners = jnp.concatenate([by_block(share, tv[c : c + 1, :]) for c in range(3)], axis=1)
    given = groups(nt(corners, vb[...]))
    around = jnp.concatenate([rx1[0, :, B:], v[...], rx1[1, :, B:]], axis=1)
    start = m[...] * v[...] - apply(around, bh, bl) * (1.0 / SCALE)
    for a in range(2):
        half = slice(a * 128, (a + 1) * 128)
        pk2[:, half] = start[:, half] + given[2 + a : 3 + a, :]
        pk2[:, V + a * 128 : V + (a + 1) * 128] = given[a : a + 1, :]
        pk2[:, 2 * V + a * 128 : 2 * V + (a + 1) * 128] = given[4 + a : 5 + a, :]

    parts2 = [send(pk2, rx2.at[i], 7 + i, chain(-o)) for i, o in enumerate((-2, -1, 1, 2, 3))]

    pl.semaphore_wait(relay_sem.at[0], 2)
    relay([z_chip(2 * HOPS), z_chip(ZG // 2 - 2 * HOPS)], 2)
    for copy in params:
        copy.wait_recv()
    build_matrix(nc, nv, nm, 1.0, flag(me < N - 2), nh, nl)
    for copy in parts2:
        copy.wait_recv()
    own_e, own_b, own_a = pk2[:, 0:V], pk2[:, V : 2 * V], pk2[:, 2 * V :]
    r_own = own_e + rx2[1, :, 2 * V :] + rx2[2, :, V : 2 * V]
    r_before = rx2[1, :, 0:V] + own_b + rx2[0, :, 2 * V :]
    r_after = rx2[2, :, 0:V] + own_a + rx2[3, :, V : 2 * V]
    r_after2 = rx2[3, :, 0:V] + rx2[2, :, 2 * V :] + rx2[4, :, V : 2 * V]
    u_own = apply(jnp.concatenate([r_before, r_own, r_after], axis=1), bh, bl)
    u_after = apply(jnp.concatenate([r_own, r_after, r_after2], axis=1), nh, nl)
    t_own = apply(jnp.concatenate([u_own, 2.0 * u_after], axis=1), bh, bl, V)

    def fold(x):
        return x[:, 0:128] + x[:, 128:256]

    products = (fold(r_own * r_own), fold(r_own * u_own), fold(u_own * u_own), fold(u_own * t_own))
    at = iota((8, 128), 0)
    stack = jnp.zeros((8, 128), F32)
    for i, p in enumerate(products):
        stack = jnp.where(at == i, p, stack)
    sums = jnp.sum(stack, axis=1, keepdims=True)
    red[0] = add_rows(jnp.where(at == iota((8, 128), 1), sums, 0.0))

    def reduce(stage, partner, order, buffer, sem):
        for j in order:
            pltpu.make_async_remote_copy(
                src_ref=red.at[stage], dst_ref=buffer.at[j - 1], send_sem=send_sem.at[sem],
                recv_sem=recv_sem.at[sem], device_id=(partner(j),), device_id_type=MESH,
            ).start()

    pl.semaphore_wait(relay_sem.at[2], 2)
    reduce(0, z_partner, Z_ORDER, red_a, 12)


    hop = column(dr[...])
    step = 16
    for c in range(0, S, step):
        here = cnew[c : c + step, :]
        raws = []
        for f in range(4):
            prob = hop[c : c + step, :] * fw[f : f + 1, :]
            mean = here * prob
            spread = jnp.sqrt(mean * (1.0 - prob))
            raw = jnp.maximum(mean + spread * dn[f, c : c + step, :].astype(F32), 0.0)
            raws.append(jnp.where(ft[f : f + 1, :] == wall, 0.0, raw))
        total = raws[0] + raws[1] + raws[2] + raws[3]
        factor = jnp.minimum(1.0, here / jnp.maximum(total, 1.0))
        for f in range(4):
            hi, lo = cut2(raws[f] * factor)
            am[c : c + step, f * T : (f + 1) * T] = hi
            am[S + c : S + c + step, f * T : (f + 1) * T] = lo
        loc[c : c + step, :] = here - total * factor
    for side in range(2):
        out = nt(ot[T + side * B : T + (side + 1) * B, :], am[...]).T
        slots[side] = out[:S, :] + out[S:, :]
    bulk = [send(slots.at[1], slots_in.at[0], 5, after), send(slots.at[0], slots_in.at[1], 6, before)]
    for w in range(0, T, 256):
        out = nt(ot[w : w + 256, :], am[...]).T
        loc[:, w : w + 256] = loc[:, w : w + 256] + out[:S, :] + out[S:, :]
    for c in range(0, T, 64):
        at = iota((64, B), 0) + c
        rt[c : c + 64, 0:B] = hot(rrow[0:1, :] == at)
        rt[c : c + 64, B:] = hot(rrow[1:2, :] == at)

    pltpu.make_async_copy(red_a, red_a, recv_sem.at[12]).wait()
    red[1] = red[0] + jnp.sum(red_a[...], axis=0)
    pl.semaphore_wait(relay_sem.at[1], 2)
    reduce(1, xy_partner, XY_ORDER, red_b, 13)

    for copy in bulk:
        copy.wait_recv()
    for side in range(2):
        hi, lo = cut2(slots_in[side])
        arr[0:S, side * B : (side + 1) * B] = hi
        arr[S:, side * B : (side + 1) * B] = lo
    for w in range(0, T, 256):
        out = nt(rt[w : w + 256, :], arr[...]).T
        cnew[:, w : w + 256] = loc[:, w : w + 256] + out[:S, :] + out[S:, :]

    out_copy = pltpu.make_async_copy(cnew, out_h, out_sem)
    out_copy.start()

    pltpu.make_async_copy(red_b, red_b, recv_sem.at[13]).wait()
    final = red[1] + jnp.sum(red_b[...], axis=0)
    rr, ru, uu, ut = (final[:, i : i + 1] for i in range(4))
    alpha0 = rr / ru
    norm1 = alpha0 * alpha0 * uu - rr
    keep = 1.0 + norm1 / rr
    curve = keep * keep * ru - 2.0 * keep * alpha0 * uu + alpha0 * alpha0 * ut
    alpha1 = norm1 / curve
    direction = keep * r_own - alpha0 * u_own
    vnew[...] = v[...] + (alpha0 * SCALE) * r_own + (alpha1 * SCALE) * direction
    for copy in sends:
        copy.wait_send()
    pltpu.make_async_copy(red_a, red_a, send_sem.at[12]).wait()
    pltpu.make_async_copy(red_b, red_b, send_sem.at[13]).wait()
    out_copy.wait()


def finish(counts_in, v_in, counts_out, v_out, hold, hold_v, in_sem, out_sem):
    rows = S // PIECES
    parts = [slice(i * rows, (i + 1) * rows) for i in range(PIECES)]
    loads = [pltpu.make_async_copy(v_in, hold_v, in_sem.at[PIECES])]
    stores = [pltpu.make_async_copy(hold_v, v_out, out_sem.at[PIECES])]
    for i, part in enumerate(parts):
        loads.append(pltpu.make_async_copy(counts_in.at[part, :], hold.at[part, :], in_sem.at[i]))
        stores.append(pltpu.make_async_copy(hold.at[part, :], counts_out.at[part, :], out_sem.at[i]))
    for copy in loads:
        copy.start()
    for load, store in zip(loads, stores):
        load.wait()
        store.start()
    for copy in stores:
        copy.wait()


def per_device(*args):
    shaped = [a.reshape(1, -1) if a.ndim == 1 else a for a in args]
    any_spec = pl.BlockSpec(memory_space=pl.ANY)
    scratch = [pltpu.VMEM(a.shape, a.dtype) for a in shaped]
    scratch += [
        pltpu.VMEM((256, T), BF16),
        pltpu.VMEM((R, 512), BF16),
        pltpu.VMEM((2 * R, T), BF16),
        pltpu.VMEM((2 * S, 4 * T), BF16),
        pltpu.VMEM((T + 2 * B, 4 * T), BF16),
        pltpu.VMEM((S, T), F32),
        pltpu.VMEM((T, 2 * B), BF16),
        pltpu.VMEM((128, 4 * T), BF16),
        pltpu.VMEM((128, 2 * B), BF16),
        pltpu.VMEM((128, T), BF16),
        pltpu.VMEM((128, 3 * T), BF16),
        pltpu.VMEM((3 * V, V), BF16),
        pltpu.VMEM((3 * V, V), BF16),
        pltpu.VMEM((3 * V, V), BF16),
        pltpu.VMEM((3 * V, V), BF16),
        pltpu.VMEM((2 * S, 2 * B), BF16),
        pltpu.VMEM((S, T), F32),
        pltpu.VMEM((2, S, B), F32),
        pltpu.VMEM((2, S, B), F32),
        pltpu.VMEM((2, 1, B + V), F32),
        pltpu.VMEM((2, 1, B + V), F32),
        pltpu.VMEM((8, V), I32),
        pltpu.VMEM((8, V), F32),
        pltpu.VMEM((1, V), F32),
        pltpu.VMEM((1, 3 * V), F32),
        pltpu.VMEM((5, 1, 3 * V), F32),
        pltpu.VMEM((2, 1, 128), F32),
        pltpu.VMEM((ZG - 1, 1, 128), F32),
        pltpu.VMEM((XY - 1, 1, 128), F32),
        pltpu.SemaphoreType.DMA((17,)),
        pltpu.SemaphoreType.DMA,
        pltpu.SemaphoreType.DMA((14,)),
        pltpu.SemaphoreType.DMA((14,)),
        pltpu.SemaphoreType.REGULAR((3,)),
    ]
    counts_new, voltage = pl.pallas_call(
        kernel,
        name="step",
        out_shape=(jax.ShapeDtypeStruct((S, T), F32), jax.ShapeDtypeStruct((1, V), F32)),
        in_specs=[any_spec] * len(shaped),
        out_specs=(any_spec, pl.BlockSpec(memory_space=pltpu.VMEM)),
        scratch_shapes=scratch,
        compiler_params=pltpu.CompilerParams(
            collective_id=1, has_side_effects=True, vmem_limit_bytes=60 * 1024 * 1024
        ),
    )(*shaped)
    counts_new, voltage = pl.pallas_call(
        finish,
        name="finish",
        out_shape=(jax.ShapeDtypeStruct((S, T), F32), jax.ShapeDtypeStruct((1, V), F32)),
        in_specs=[any_spec, any_spec],
        out_specs=(any_spec, any_spec),
        scratch_shapes=[
            pltpu.VMEM((S, T), F32),
            pltpu.VMEM((1, V), F32),
            pltpu.SemaphoreType.DMA((PIECES + 1,)),
            pltpu.SemaphoreType.DMA((PIECES + 1,)),
        ],
        compiler_params=pltpu.CompilerParams(vmem_limit_bytes=60 * 1024 * 1024),
    )(counts_new, voltage)
    return counts_new, voltage.reshape(-1)


def solution(mesh):
    placed = (
        P(None, "dom"), P(), P(), P(), P(None, "dom"), P(), P(None, "dom"), P(None, "dom"), P(None, "dom"),
        P(None, None, "dom"), P("dom"), P(None, "dom"), P("dom"), P("dom"), P("dom"), P(None, "dom"),
        P(None, "dom"),
    )
    return jax.shard_map(
        per_device, mesh=mesh, in_specs=placed, out_specs=(P(None, "dom"), P("dom")), check_vma=False
    )
```
